32 devices in a mesh: ctx: 8 (over y, x, core), head: 4 (over z).
Axes of the slice: x: 2, y: 2, z: 4, core: 2. Of those that a mesh axis runs over, the one named last changes fastest.
Arguments:
- query_proj: bfloat16 [4096, 2048], P('ctx', 'head'), may hold values from -32 to 32
- projected_keys: bfloat16 [4096, 1024], P('ctx', 'head'), may hold values from -32 to 32
- projected_values: bfloat16 [4096, 1024], P('ctx', 'head'), may hold values from -12 to 12
- w_out: bfloat16 [2048, 4096], P('head'), may hold values from -0.1875 to 0.1875
- attended_blocks: int32 [8, 8], replicated, may hold values from -1 to 7, as said below
- grad_out: bfloat16 [4096, 4096], P('ctx', 'head'), may hold values from -6 to 6
Outputs:
- layer_out: bfloat16 [4096, 4096], P('ctx', 'head')
- grad_query: float32 [4096, 2048], P('ctx', 'head')
- grad_key: float32 [4096, 1024], P('ctx', 'head')
- grad_value: float32 [4096, 1024], P('ctx', 'head')
- grad_wout: float32 [2048, 4096], P('head', 'ctx')
The draws below stay inside these ranges and needn't reach their ends.
Inputs may be any that keep to these rules, and one draw needn't show every extreme that they name: `attended_blocks`: row b lists key blocks: its first entry is b; if b >= 4 its second entry is b - 4; the other live entries are distinct blocks among b - 7 to b - 1; -1 fills the unused entries. Row b has between min(2, b + 1) and 8 live entries, and some row has exactly 8.
All inputs are finite; a program needn't handle non-finite values.
Results may differ from the reference program's by a relative error of at most 0.04.
Values may be sent and summed in bfloat16 or wider, within the bound.
A program may use at most 128 MiB of HBM per device.

```python
import jax
import jax.numpy as jnp
from jax import lax

D = 4096
QUERY_HEADS = 16
KEY_VALUE_HEADS = 8
HEAD_SIZE = 128
BLOCK_TOKENS = 512
BLK_DEV = 1
SEGMENT_BLOCKS = 8
SEGMENT_TOKENS = 4096
LIST = 8
N_CTX = 8
N_HEAD = 4


def drawn(key):
    base_key = jax.random.fold_in(key, 907)
    query_key, random_keys_seed = jax.random.split(base_key, 2)
    query_matrix = 2.0 * jax.random.truncated_normal(query_key, -3.0, 3.0, (SEGMENT_TOKENS, QUERY_HEADS * HEAD_SIZE), jnp.float32)
    returned_keys = jax.random.truncated_normal(random_keys_seed, -4.0, 4.0, (SEGMENT_TOKENS, KEY_VALUE_HEADS * HEAD_SIZE), jnp.float32)
    return (query_matrix, returned_keys)


def draw_query_proj(key, part):
    return drawn(key)[0].astype(jnp.bfloat16)


def draw_projected_keys(key, part):
    return drawn(key)[1].astype(jnp.bfloat16)


def draw_attended_blocks(key, part):
    base_key = jax.random.fold_in(key, 311)
    first_key, second_key, force_key, score_key = jax.random.split(base_key, 4)
    first_draw = jax.random.randint(first_key, (SEGMENT_BLOCKS,), 0, 11)
    second_draw = jax.random.randint(second_key, (SEGMENT_BLOCKS,), 0, 11)
    wanted = 2 + first_draw * second_draw // 10
    blocks = jnp.arange(SEGMENT_BLOCKS, dtype=jnp.int32)
    forced = jax.random.randint(force_key, (), LIST - 1, SEGMENT_BLOCKS)
    wanted = jnp.where(blocks == forced, LIST, wanted)
    lengths = jnp.minimum(jnp.minimum(wanted, LIST), blocks + 1)
    far_block = blocks - SEGMENT_BLOCKS // 2
    has_far = far_block >= 0
    raw_scores = jax.random.randint(score_key, (SEGMENT_BLOCKS, SEGMENT_BLOCKS), 0, 1 << 20)
    excluded = (blocks[None, :] >= blocks[:, None]) | (blocks[None, :] < blocks[:, None] - (LIST - 1)) | (blocks[None, :] == far_block[:, None])
    ranked = jnp.where(excluded, -1, raw_scores * SEGMENT_BLOCKS + blocks[None, :])
    picked_scores, chosen = lax.top_k(ranked, LIST - 1)
    chosen = chosen.astype(jnp.int32)
    with_far = jnp.concatenate([far_block[:, None], chosen[:, :LIST - 2]], 1)
    candidates = jnp.where(has_far[:, None], with_far, chosen)
    slot_ids = jnp.arange(LIST - 1, dtype=jnp.int32)[None, :]
    earlier = jnp.where(slot_ids < (lengths - 1)[:, None], candidates, -1)
    return jnp.concatenate([blocks[:, None], earlier], 1).astype(jnp.int32)


def raised(entries, key, source, target, blocks, factor):
    def block_of(axis_at):
        return (jnp.arange(entries.shape[axis_at]) // (entries.shape[axis_at] // blocks)).reshape((-1,) + (1,) * (entries.ndim - 1 - axis_at))

    near = jax.random.permutation(key, blocks)[block_of(target)]
    other_side = (block_of(target) + blocks // 2) % blocks
    return jnp.where((block_of(source) == near) | (block_of(source) == other_side), factor * entries, entries)


def level_of(own_key, dims, cuts, low, top_value):
    level = 1.0
    for dim, parts in cuts:
        steps = jax.random.uniform(jax.random.fold_in(jax.random.fold_in(own_key, 6), dim), (parts,), jnp.float32, low / len(cuts), top_value / len(cuts))
        level = level * jnp.repeat(jnp.exp(steps), dims[dim] // parts).reshape((-1,) + (1,) * (len(dims) - 1 - dim))
    return level


def gaussian(own_key, dims, scale, reach, shards=(), kind=jnp.bfloat16):
    drawn = jax.random.normal(own_key, dims, jnp.float32) * scale
    if len(shards) > 0:
        drawn = level_of(own_key, dims, shards, -0.22, 0.18) * drawn
    return jnp.clip(drawn, min=-reach, max=reach).astype(kind)


def heavy_noise(own_key, extent, spread, bound, cuts, heavy, kind=jnp.bfloat16):
    values = spread * jax.random.normal(own_key, extent, jnp.float32)
    if cuts:
        values = values * level_of(own_key, extent, cuts, -0.22, 0.18)
    return jnp.clip(raised(values, jax.random.fold_in(own_key, 3), *heavy), -bound, bound).astype(kind)


def setup_inputs(seed: int = 0) -> dict:
    keys = jax.random.split(jax.random.key(seed), 7)
    query_proj = draw_query_proj(jax.random.fold_in(keys[6], 71), 0)
    projected_keys = draw_projected_keys(jax.random.fold_in(keys[6], 71), 0)
    projected_values = gaussian(keys[2], (SEGMENT_TOKENS, KEY_VALUE_HEADS * HEAD_SIZE), 2.0, 12.0, ((0, 8), (1, 4)))
    w_out = heavy_noise(keys[3], (QUERY_HEADS * HEAD_SIZE, D), (QUERY_HEADS * HEAD_SIZE) ** -0.5, 0.1875, ((0, 4),), (0, 1, 4, 2.0))
    attended_blocks = draw_attended_blocks(jax.random.fold_in(keys[6], 71), 0)
    grad_out = heavy_noise(keys[5], (SEGMENT_TOKENS, D), 1.0, 6.0, ((0, 8), (1, 4)), (0, 1, 8, 2.0))
    return {"query_proj": query_proj, "projected_keys": projected_keys, "projected_values": projected_values, "w_out": w_out, "attended_blocks": attended_blocks, "grad_out": grad_out}


def load_key_block(source, key_block_index, kv_heads):
    rows_per_block = lax.dynamic_slice_in_dim(source, key_block_index * BLOCK_TOKENS, BLOCK_TOKENS, 0)
    return rows_per_block.reshape(BLOCK_TOKENS, kv_heads, HEAD_SIZE).astype(jnp.float32)


def causal_scores(query_portion, key_row_slice, key_block_index, diagonal_block):
    raw_scores = jnp.einsum('ikgd,jkd->kgij', query_portion, key_row_slice) * (HEAD_SIZE ** -0.5)
    row_pos = lax.broadcasted_iota(jnp.int32, (BLOCK_TOKENS, BLOCK_TOKENS), 0)
    col_pos = lax.broadcasted_iota(jnp.int32, (BLOCK_TOKENS, BLOCK_TOKENS), 1)
    allowed = (key_block_index < diagonal_block) | (col_pos <= row_pos)
    return jnp.where(allowed, raw_scores, -jnp.inf)


def rounded(values):
    low_values = lax.optimization_barrier(values.astype(jnp.bfloat16))
    return low_values.astype(jnp.float32)


def reference(query_proj, projected_keys, projected_values, w_out, attended_blocks, grad_out):
    heads_per_group = QUERY_HEADS // KEY_VALUE_HEADS
    slot_count = attended_blocks.shape[1]
    score_scale = HEAD_SIZE ** -0.5
    head_cols = QUERY_HEADS * HEAD_SIZE // N_HEAD
    range_rows = SEGMENT_TOKENS // N_CTX
    key_column_span = KEY_VALUE_HEADS * HEAD_SIZE

    def heads_of(source, diagonal_block):
        rows_per_block = lax.dynamic_slice_in_dim(source, diagonal_block * BLOCK_TOKENS, BLOCK_TOKENS, 0)
        return rows_per_block.reshape(BLOCK_TOKENS, KEY_VALUE_HEADS, heads_per_group, HEAD_SIZE).astype(jnp.float32)

    def forward_block(diagonal_block):
        listed = attended_blocks[diagonal_block]
        query_portion = heads_of(query_proj, diagonal_block)

        def opening_sweep(slot_num, running):
            key_block_index = listed[slot_num]

            def live(present_block):
                running_largest, softmax_denominator = present_block
                score_matrix = causal_scores(query_portion, load_key_block(projected_keys, key_block_index, KEY_VALUE_HEADS), key_block_index, diagonal_block)
                new_largest = jnp.maximum(running_largest, jnp.max(score_matrix, -1))
                softmax_denominator = softmax_denominator * jnp.exp(running_largest - new_largest) + jnp.sum(jnp.exp(score_matrix - new_largest[..., None]), -1)
                return new_largest, softmax_denominator

            return lax.cond(key_block_index >= 0, live, lambda present_block: present_block, running)

        initial_state = (jnp.full((KEY_VALUE_HEADS, heads_per_group, BLOCK_TOKENS), -jnp.inf, jnp.float32), jnp.zeros((KEY_VALUE_HEADS, heads_per_group, BLOCK_TOKENS), jnp.float32))
        running_largest, softmax_denominator = lax.fori_loop(0, slot_count, opening_sweep, initial_state)

        def closing_sweep(slot_num, weighted_values):
            key_block_index = listed[slot_num]

            def live(present_block):
                score_matrix = causal_scores(query_portion, load_key_block(projected_keys, key_block_index, KEY_VALUE_HEADS), key_block_index, diagonal_block)
                attention_weights = rounded(jnp.exp(score_matrix - running_largest[..., None]))
                return present_block + jnp.einsum('mayf,fmb->mayb', attention_weights, load_key_block(projected_values, key_block_index, KEY_VALUE_HEADS))

            return lax.cond(key_block_index >= 0, live, lambda present_block: present_block, weighted_values)

        weighted_values = lax.fori_loop(0, slot_count, closing_sweep, jnp.zeros((KEY_VALUE_HEADS, heads_per_group, BLOCK_TOKENS, HEAD_SIZE), jnp.float32))
        attn_block = (weighted_values / softmax_denominator[..., None]).astype(jnp.bfloat16)
        attn_block = attn_block.transpose(2, 0, 1, 3).reshape(BLOCK_TOKENS, QUERY_HEADS * HEAD_SIZE)
        return attn_block, running_largest + jnp.log(softmax_denominator)

    attn_blocks, log_totals = lax.map(forward_block, jnp.arange(SEGMENT_BLOCKS, dtype=jnp.int32))
    attention = attn_blocks.reshape(SEGMENT_TOKENS, QUERY_HEADS * HEAD_SIZE)

    def add_group(out_sum, group_index):
        column_part = lax.dynamic_slice_in_dim(attention, group_index * head_cols, head_cols, 1)
        row_part = lax.dynamic_slice_in_dim(w_out, group_index * head_cols, head_cols, 0)
        return out_sum + rounded(jnp.dot(column_part, row_part, preferred_element_type=jnp.float32)), None

    out_sum, unused = lax.scan(add_group, jnp.zeros((SEGMENT_TOKENS, D), jnp.float32), jnp.arange(N_HEAD, dtype=jnp.int32))
    layer_out = out_sum.astype(jnp.bfloat16)

    grad_attn = jnp.dot(grad_out, w_out.T, preferred_element_type=jnp.float32).astype(jnp.bfloat16)

    def add_range(weight_sum, range_index):
        attn_rows = lax.dynamic_slice_in_dim(attention, range_index * range_rows, range_rows, 0)
        grad_rows = lax.dynamic_slice_in_dim(grad_out, range_index * range_rows, range_rows, 0)
        term = lax.dot_general(attn_rows, grad_rows, (((0,), (0,)), ((), ())), preferred_element_type=jnp.float32)
        return weight_sum + rounded(term), None

    grad_wout, unused = lax.scan(add_range, jnp.zeros((QUERY_HEADS * HEAD_SIZE, D), jnp.float32), jnp.arange(N_CTX, dtype=jnp.int32))

    def backward_block(diagonal_block, key_part, value_part):
        listed = attended_blocks[diagonal_block]
        query_portion = heads_of(query_proj, diagonal_block)
        grad_heads = heads_of(grad_attn, diagonal_block)
        attn_heads = heads_of(attention, diagonal_block)
        delta = jnp.einsum('ikgd,ikgd->kgi', grad_heads, attn_heads)
        log_total = log_totals[diagonal_block]

        def forward_visit(slot_num, running):
            key_block_index = listed[slot_num]

            def live(present_block):
                query_gradient_total, key_increments, value_increments = present_block
                key_row_slice = load_key_block(projected_keys, key_block_index, KEY_VALUE_HEADS)
                value_row_slice = load_key_block(projected_values, key_block_index, KEY_VALUE_HEADS)
                score_matrix = causal_scores(query_portion, key_row_slice, key_block_index, diagonal_block)
                probs = jnp.exp(score_matrix - log_total[..., None])
                grad_probs = jnp.einsum('ikgd,jkd->kgij', grad_heads, value_row_slice)
                grad_scores = rounded(score_scale * probs * (grad_probs - delta[..., None]))
                query_gradient_total = query_gradient_total + jnp.einsum('mayf,fmb->mayb', grad_scores, key_row_slice)
                key_add = jnp.einsum('kgij,ikgd->jkd', grad_scores, query_portion).reshape(BLOCK_TOKENS, key_column_span)
                value_add = jnp.einsum('kgij,ikgd->jkd', rounded(probs), grad_heads).reshape(BLOCK_TOKENS, key_column_span)
                key_increments = lax.dynamic_update_index_in_dim(key_increments, key_add, slot_num, 0)
                value_increments = lax.dynamic_update_index_in_dim(value_increments, value_add, slot_num, 0)
                return query_gradient_total, key_increments, value_increments

            return lax.cond(key_block_index >= 0, live, lambda present_block: present_block, running)

        initial_state = (jnp.zeros((KEY_VALUE_HEADS, heads_per_group, BLOCK_TOKENS, HEAD_SIZE), jnp.float32), jnp.zeros((slot_count, BLOCK_TOKENS, key_column_span), jnp.float32), jnp.zeros((slot_count, BLOCK_TOKENS, key_column_span), jnp.float32))
        query_gradient_total, key_increments, value_increments = lax.fori_loop(0, slot_count, forward_visit, initial_state)
        target_blocks = jnp.where(listed >= 0, listed, diagonal_block).astype(jnp.int32)
        key_part = key_part.reshape(SEGMENT_BLOCKS, BLOCK_TOKENS, key_column_span).at[target_blocks].add(key_increments).reshape(SEGMENT_TOKENS, key_column_span)
        value_part = value_part.reshape(SEGMENT_BLOCKS, BLOCK_TOKENS, key_column_span).at[target_blocks].add(value_increments).reshape(SEGMENT_TOKENS, key_column_span)
        return query_gradient_total.transpose(2, 0, 1, 3).reshape(BLOCK_TOKENS, QUERY_HEADS * HEAD_SIZE), key_part, value_part

    def range_grads(totals, range_index):
        key_part = jnp.zeros((SEGMENT_TOKENS, key_column_span), jnp.float32)
        value_part = jnp.zeros((SEGMENT_TOKENS, key_column_span), jnp.float32)
        query_rows = []
        for local_block in range(BLK_DEV):
            diagonal_block = (range_index * BLK_DEV + local_block).astype(jnp.int32)
            query_block, key_part, value_part = backward_block(diagonal_block, key_part, value_part)
            query_rows.append(query_block)
        return (totals[0] + rounded(key_part), totals[1] + rounded(value_part)), jnp.concatenate(query_rows, 0)

    start_totals = (jnp.zeros((SEGMENT_TOKENS, key_column_span), jnp.float32), jnp.zeros((SEGMENT_TOKENS, key_column_span), jnp.float32))
    totals, query_ranges = lax.scan(range_grads, start_totals, jnp.arange(N_CTX, dtype=jnp.int32))
    grad_query = query_ranges.reshape(SEGMENT_TOKENS, QUERY_HEADS * HEAD_SIZE)
    return (layer_out, grad_query, totals[0], totals[1], grad_wout)
```

```python
import functools
import math

import jax
import jax.numpy as jnp
from jax import lax
from jax.experimental import pallas as pl
from jax.experimental.pallas import tpu as pltpu
from jax.sharding import PartitionSpec as P

HEAD_SIZE = 128
BLOCK_TOKENS = 512


def shifted(value, axis, steps):
    count = lax.axis_size(axis)
    leading, last = (max(0, -steps), min(count, count - steps))
    return lax.ppermute(value, axis, [(source, source + steps) for source in range(leading, last)])


def load_key_block(source, local_index, kv_heads):
    rows_per_block = lax.dynamic_slice_in_dim(source, local_index * BLOCK_TOKENS, BLOCK_TOKENS, 0)
    return rows_per_block.reshape(BLOCK_TOKENS, kv_heads, HEAD_SIZE)


def causal_scores(query_portion, key_row_slice, key_block_index, diagonal_block):
    raw_scores = jnp.einsum(
        "ikgd,jkd->kgij", query_portion, key_row_slice, preferred_element_type=jnp.float32
    ) * HEAD_SIZE ** (-0.5)
    row_pos = lax.broadcasted_iota(jnp.int32, (BLOCK_TOKENS, BLOCK_TOKENS), 0)
    col_pos = lax.broadcasted_iota(jnp.int32, (BLOCK_TOKENS, BLOCK_TOKENS), 1)
    allowed = (key_block_index < diagonal_block) | (col_pos <= row_pos)
    return jnp.where(allowed, raw_scores, -jnp.inf)


def general_device(query_proj, projected_keys, projected_values, w_out, attended_blocks, grad_out):
    ctx_rank = lax.axis_index("ctx")
    ctx_count = lax.axis_size("ctx")
    local_rows = query_proj.shape[0]
    blocks_here = local_rows // BLOCK_TOKENS
    kv_heads = projected_keys.shape[1] // HEAD_SIZE
    key_column_span = projected_keys.shape[1]
    head_cols = query_proj.shape[1]
    heads_per_group = head_cols // HEAD_SIZE // kv_heads
    slot_count = attended_blocks.shape[1]
    score_scale = HEAD_SIZE ** (-0.5)
    reach = min((slot_count - 1 + blocks_here - 1) // blocks_here, ctx_count - 1)
    margin_rows = reach * local_rows
    far_step = ctx_count // 2
    use_far = far_step > reach
    window_rows = margin_rows + local_rows
    front_rows = max(reach, far_step) * local_rows
    all_keys, all_values = (
        lax.all_gather(projected_keys, "ctx", axis=0, tiled=True),
        lax.all_gather(projected_values, "ctx", axis=0, tiled=True),
    )
    total_rows = all_keys.shape[0]

    def heads_of(source):
        return source.reshape(BLOCK_TOKENS, kv_heads, heads_per_group, HEAD_SIZE)

    local_block = 0
    diagonal_block = ctx_rank * blocks_here + local_block
    listed = lax.dynamic_index_in_dim(attended_blocks, diagonal_block, 0, keepdims=False)
    query_portion = heads_of(query_proj)

    def forward_visit(slot_num, running):
        key_block_index = listed[slot_num]

        def forward_live(present_block):
            running_largest, softmax_denominator, weighted_values = present_block
            score_matrix = causal_scores(
                query_portion,
                load_key_block(all_keys, key_block_index, kv_heads),
                key_block_index,
                diagonal_block,
            )
            new_largest = jnp.maximum(running_largest, jnp.max(score_matrix, -1))
            rescale = jnp.exp(running_largest - new_largest)
            attention_weights = jnp.exp(score_matrix - new_largest[..., None])
            softmax_denominator = softmax_denominator * rescale + jnp.sum(attention_weights, -1)
            value_row_slice = load_key_block(all_values, key_block_index, kv_heads)
            weighted_values = weighted_values * rescale[..., None] + jnp.einsum(
                "mayf,fmb->mayb",
                attention_weights.astype(jnp.bfloat16),
                value_row_slice,
                preferred_element_type=jnp.float32,
            )
            return (new_largest, softmax_denominator, weighted_values)

        return lax.cond(
            key_block_index >= 0, forward_live, lambda present_block: present_block, running
        )

    initial_state = (
        jnp.full((kv_heads, heads_per_group, BLOCK_TOKENS), -jnp.inf, jnp.float32),
        jnp.zeros((kv_heads, heads_per_group, BLOCK_TOKENS), jnp.float32),
        jnp.zeros((kv_heads, heads_per_group, BLOCK_TOKENS, HEAD_SIZE), jnp.float32),
    )
    running_largest, softmax_denominator, weighted_values = lax.fori_loop(
        0, slot_count, forward_visit, initial_state
    )
    attn_block = (weighted_values / softmax_denominator[..., None]).astype(jnp.bfloat16)
    attn_parts = attn_block.transpose(2, 0, 1, 3).reshape(BLOCK_TOKENS, head_cols)
    log_totals = [running_largest + jnp.log(softmax_denominator)]
    out_terms = jnp.dot(attn_parts, w_out, preferred_element_type=jnp.float32)
    layer_out = lax.psum_scatter(
        out_terms.astype(jnp.bfloat16), "head", scatter_dimension=1, tiled=True
    )
    piece = lax.all_gather(grad_out, "head", axis=1, tiled=True)
    grad_sum = lax.dot_general(
        piece, w_out, (((1,), (1,)), ((), ())), preferred_element_type=jnp.float32
    )
    column_term = lax.dot_general(
        attn_parts, piece, (((0,), (0,)), ((), ())), preferred_element_type=jnp.float32
    )
    weight_terms = column_term
    grad_sum, weight_terms = (grad_sum, weight_terms)
    grad_attn = grad_sum.astype(jnp.bfloat16)
    grad_wout = lax.psum_scatter(
        weight_terms.astype(jnp.bfloat16), "ctx", scatter_dimension=1, tiled=True
    ).astype(jnp.float32)
    key_gradient_totals = jnp.zeros((total_rows, key_column_span), jnp.float32)
    value_gradient_totals = jnp.zeros((total_rows, key_column_span), jnp.float32)
    local_block = 0
    diagonal_block = ctx_rank * blocks_here + local_block
    listed = lax.dynamic_index_in_dim(attended_blocks, diagonal_block, 0, keepdims=False)
    query_portion = heads_of(query_proj)
    grad_heads = heads_of(grad_attn)
    attn_heads = heads_of(attn_parts)
    delta = jnp.einsum("ikgd,ikgd->kgi", grad_heads, attn_heads, preferred_element_type=jnp.float32)
    log_total = log_totals[local_block]

    def reverse_visit(slot_num, running):
        key_block_index = listed[slot_num]

        def reverse_live(present_block):
            query_gradient_total, key_buffer, value_buffer = present_block
            key_row_slice = load_key_block(all_keys, key_block_index, kv_heads)
            value_row_slice = load_key_block(all_values, key_block_index, kv_heads)
            score_matrix = causal_scores(
                query_portion, key_row_slice, key_block_index, diagonal_block
            )
            probs = jnp.exp(score_matrix - log_total[..., None])
            grad_probs = jnp.einsum(
                "ikgd,jkd->kgij", grad_heads, value_row_slice, preferred_element_type=jnp.float32
            )
            grad_scores = (score_scale * probs * (grad_probs - delta[..., None])).astype(
                jnp.bfloat16
            )
            query_gradient_total = query_gradient_total + jnp.einsum(
                "mayf,fmb->mayb", grad_scores, key_row_slice, preferred_element_type=jnp.float32
            )
            key_add = jnp.einsum(
                "kgij,ikgd->jkd", grad_scores, query_portion, preferred_element_type=jnp.float32
            ).reshape(BLOCK_TOKENS, -1)
            value_add = jnp.einsum(
                "kgij,ikgd->jkd",
                probs.astype(jnp.bfloat16),
                grad_heads,
                preferred_element_type=jnp.float32,
            ).reshape(BLOCK_TOKENS, -1)
            begin = key_block_index * BLOCK_TOKENS
            key_buffer = lax.dynamic_update_slice_in_dim(
                key_buffer,
                lax.dynamic_slice_in_dim(key_buffer, begin, BLOCK_TOKENS, 0) + key_add,
                begin,
                0,
            )
            value_buffer = lax.dynamic_update_slice_in_dim(
                value_buffer,
                lax.dynamic_slice_in_dim(value_buffer, begin, BLOCK_TOKENS, 0) + value_add,
                begin,
                0,
            )
            return (query_gradient_total, key_buffer, value_buffer)

        return lax.cond(
            key_block_index >= 0, reverse_live, lambda present_block: present_block, running
        )

    initial_state = (
        jnp.zeros((kv_heads, heads_per_group, BLOCK_TOKENS, HEAD_SIZE), jnp.float32),
        key_gradient_totals,
        value_gradient_totals,
    )
    query_gradient_total, key_gradient_totals, value_gradient_totals = lax.fori_loop(
        0, slot_count, reverse_visit, initial_state
    )
    query_grads = query_gradient_total.transpose(2, 0, 1, 3).reshape(BLOCK_TOKENS, head_cols)

    def to_window(buffer):
        padded = jnp.concatenate([jnp.zeros((front_rows, key_column_span), jnp.float32), buffer], 0)
        window_part = lax.dynamic_slice_in_dim(
            padded, front_rows - margin_rows + ctx_rank * local_rows, window_rows, 0
        )
        if use_far:
            far_part = lax.dynamic_slice_in_dim(
                padded, front_rows + (ctx_rank - far_step) * local_rows, local_rows, 0
            )
            return jnp.concatenate([window_part, far_part], 0)
        return window_part

    low_keys = to_window(key_gradient_totals).astype(jnp.bfloat16)
    low_values = to_window(value_gradient_totals).astype(jnp.bfloat16)
    grad_key = low_keys[margin_rows:window_rows].astype(jnp.float32)
    grad_value = low_values[margin_rows:window_rows].astype(jnp.float32)
    for distance in range(1, reach + 1):
        begin = (reach - distance) * local_rows
        back_keys, back_values = shifted(
            (low_keys[begin : begin + local_rows], low_values[begin : begin + local_rows]),
            "ctx",
            -distance,
        )
        grad_key = grad_key + back_keys.astype(jnp.float32)
        grad_value = grad_value + back_values.astype(jnp.float32)
    if use_far:
        far_back_keys, far_back_values = shifted(
            (low_keys[window_rows:], low_values[window_rows:]), "ctx", -far_step
        )
        grad_key = grad_key + far_back_keys.astype(jnp.float32)
        grad_value = grad_value + far_back_values.astype(jnp.float32)
    return (layer_out, query_grads, grad_key, grad_value, grad_wout)


MESH = pl.DeviceIdType.MESH
VMEM_BYTES = 48 * 1024 * 1024
EXP2_SCALE = HEAD_SIZE ** (-0.5) * math.log2(math.e)
CONTRACT_LAST = (((1,), (1,)), ((), ()))
CONTRACT_FIRST = (((0,), (0,)), ((), ()))


def dot(left, right, dims=(((1,), (0,)), ((), ()))):
    return lax.dot_general(left, right, dims, preferred_element_type=jnp.float32)


def greet(peers, count):
    barrier = pltpu.get_barrier_semaphore()
    for peer in peers:
        pl.semaphore_signal(barrier, inc=1, device_id={"ctx": peer}, device_id_type=MESH)
    pl.semaphore_wait(barrier, count)


def remote(source, target, send_sem, recv_sem, peer):
    return pltpu.make_async_remote_copy(
        src_ref=source,
        dst_ref=target,
        send_sem=send_sem,
        recv_sem=recv_sem,
        device_id={"ctx": peer},
        device_id_type=MESH,
    )


def spread_kernel(count, kv_ref, q_ref, kv_all, q_units, send, recv, q_send, q_recv, local):
    me = lax.axis_index("ctx")
    core = lax.rem(me, 2)
    sibling = me + 1 - 2 * core
    across = count - 2 - (me - core)
    greet([lax.rem(me + step, count) for step in range(1, count)], count - 1)
    copies = []
    for step in range(1, count):
        peer = lax.rem(me + step, count)
        copy = remote(
            kv_ref.at[lax.rem(peer, 2)], kv_all.at[me], send.at[step], recv.at[step], peer
        )
        copy.start()
        copies.append(copy)

    @pl.when(core == 0)
    def _():
        remote(q_ref.at[1], q_units.at[0], q_send.at[0], q_recv.at[0], sibling).start()
        mine = pltpu.make_async_copy(q_ref.at[0], q_units.at[0], local.at[1])
        mine.start()
        mine.wait()

    @pl.when(core == 1)
    def _():
        remote(q_ref.at[0], q_units.at[1], q_send.at[0], q_recv.at[1], across).start()
        remote(q_ref.at[1], q_units.at[1], q_send.at[1], q_recv.at[1], across + 1).start()

    mine = pltpu.make_async_copy(kv_ref.at[core], kv_all.at[me], local.at[0])
    mine.start()
    mine.wait()
    for copy in copies:
        copy.wait()

    remote(q_ref.at[0], q_units.at[1], q_send.at[0], q_recv.at[1], across).wait()

    @pl.when(core == 1)
    def _():
        remote(q_ref.at[1], q_units.at[0], q_send.at[1], q_recv.at[0], sibling).wait()


def return_kernel(count, dkv_ref, dq_ref, dkv_all, dq_halves, send, recv, q_send, q_recv, local):
    me = lax.axis_index("ctx")
    core = lax.rem(me, 2)
    sibling = me + 1 - 2 * core
    across = count - 2 - (me - core)
    greet([lax.rem(me + step, count) for step in range(1, count)], count - 1)
    copies = []
    for step in range(1, count):
        peer = lax.rem(me + step, count)
        copy = remote(dkv_ref.at[peer], dkv_all.at[me], send.at[step], recv.at[step], peer)
        copy.start()
        copies.append(copy)
    remote(dq_ref.at[1], dq_halves.at[core], q_send.at[0], q_recv.at[core], across + 1).start()

    @pl.when(core == 1)
    def _():
        remote(dq_ref.at[0], dq_halves.at[1], q_send.at[1], q_recv.at[1], sibling).start()

    @pl.when(core == 0)
    def _():
        mine = pltpu.make_async_copy(dq_ref.at[0], dq_halves.at[0], local.at[1])
        mine.start()
        mine.wait()

    mine = pltpu.make_async_copy(dkv_ref.at[me], dkv_all.at[me], local.at[0])
    mine.start()
    mine.wait()
    for copy in copies:
        copy.wait()
    remote(dq_ref.at[1], dq_halves.at[1], q_send.at[0], q_recv.at[1], across + 1).wait()

    @pl.when(core == 1)
    def _():
        remote(dq_ref.at[0], dq_halves.at[0], q_send.at[1], q_recv.at[0], across).wait()


def exchange(body, collective_id, count, blocks, units):
    any_space = pl.BlockSpec(memory_space=pl.ANY)
    return pl.pallas_call(
        functools.partial(body, count),
        out_shape=(
            jax.ShapeDtypeStruct((count,) + blocks.shape[1:], blocks.dtype),
            jax.ShapeDtypeStruct(units.shape, units.dtype),
        ),
        in_specs=[any_space, any_space],
        out_specs=(any_space, any_space),
        scratch_shapes=[
            pltpu.SemaphoreType.DMA((count,)),
            pltpu.SemaphoreType.DMA((count,)),
            pltpu.SemaphoreType.DMA((2,)),
            pltpu.SemaphoreType.DMA((2,)),
            pltpu.SemaphoreType.DMA((2,)),
        ],
        compiler_params=pltpu.CompilerParams(
            collective_id=collective_id, has_side_effects=True, vmem_limit_bytes=VMEM_BYTES
        ),
        cost_estimate=pl.CostEstimate(
            flops=0, bytes_accessed=2 * blocks.size * 2 + units.size * 4, transcendentals=0
        ),
    )(blocks, units)


def head_part(value, head):
    return value[:, head * HEAD_SIZE : (head + 1) * HEAD_SIZE]


def diagonal_mask(scores):
    key_row = lax.broadcasted_iota(jnp.int32, scores.shape, 0)
    query_col = lax.broadcasted_iota(jnp.int32, scores.shape, 1)
    return jnp.where(key_row <= query_col, scores, -jnp.inf)


def forward_kernel(rows_ref, q_ref, kv_ref, attn_ref, total_ref, largest, denominator, weighted):
    unit = pl.program_id(0)
    heads = q_ref.shape[2] // HEAD_SIZE

    def visit(block, diagonal):
        keys = kv_ref[block, :, :HEAD_SIZE]
        values = kv_ref[block, :, HEAD_SIZE:]
        for head in range(heads):
            at = pl.ds(head, 1)
            scores = dot(keys, head_part(q_ref[0], head), CONTRACT_LAST)
            if diagonal:
                scores = diagonal_mask(scores)
            top = jnp.max(scores, 0, keepdims=True)
            if not diagonal:
                before = largest[at, :]
                top = jnp.maximum(before, top)
                rescale = jnp.exp2((before - top) * EXP2_SCALE)
            weights = jnp.exp2(scores * EXP2_SCALE - top * EXP2_SCALE)
            added = jnp.sum(weights, 0, keepdims=True)
            product = dot(values, weights.astype(jnp.bfloat16), CONTRACT_FIRST)
            largest[at, :] = top
            if diagonal:
                denominator[at, :] = added
                weighted[head] = product
            else:
                denominator[at, :] = denominator[at, :] * rescale + added
                weighted[head] = weighted[head] * rescale + product

    visit(rows_ref[unit, 0], True)

    @pl.loop(1, rows_ref.shape[1])
    def _(slot):
        block = rows_ref[unit, slot]

        @pl.when(block >= 0)
        def _():
            visit(block, False)

    for head in range(heads):
        at = pl.ds(head, 1)
        bottom = denominator[at, :]
        attn_ref[0, :, head * HEAD_SIZE : (head + 1) * HEAD_SIZE] = (
            (weighted[head] / bottom).T.astype(jnp.bfloat16)
        )
        total_ref[0, at, :] = largest[at, :] * EXP2_SCALE + jnp.log2(bottom)


def forward_units(rows, q_units, kv_all):
    units, tokens, width = q_units.shape
    heads = width // HEAD_SIZE
    whole = pl.BlockSpec(kv_all.shape, lambda unit, rows: (0, 0, 0))
    per_unit = pl.BlockSpec((1, tokens, width), lambda unit, rows: (unit, 0, 0))
    per_total = pl.BlockSpec((1, heads, tokens), lambda unit, rows: (unit, 0, 0))
    return pl.pallas_call(
        forward_kernel,
        grid_spec=pltpu.PrefetchScalarGridSpec(
            num_scalar_prefetch=1,
            grid=(units,),
            in_specs=[per_unit, whole],
            out_specs=(per_unit, per_total),
            scratch_shapes=[
                pltpu.VMEM((heads, tokens), jnp.float32),
                pltpu.VMEM((heads, tokens), jnp.float32),
                pltpu.VMEM((heads, HEAD_SIZE, tokens), jnp.float32),
            ],
        ),
        out_shape=(
            jax.ShapeDtypeStruct(q_units.shape, jnp.bfloat16),
            jax.ShapeDtypeStruct((units, heads, tokens), jnp.float32),
        ),
        compiler_params=pltpu.CompilerParams(vmem_limit_bytes=VMEM_BYTES),
        cost_estimate=pl.CostEstimate(
            flops=20 * tokens * tokens * width,
            bytes_accessed=kv_all.size * 2,
            transcendentals=5 * tokens * tokens * heads,
        ),
    )(rows, q_units, kv_all)


def backward_kernel(
    rows_ref, q_ref, g_ref, attn_ref, total_ref, kv_ref, dq_ref, dkv_ref, delta, dq_sum, dkv_sum
):
    unit = pl.program_id(0)
    heads = q_ref.shape[2] // HEAD_SIZE
    score_scale = HEAD_SIZE ** (-0.5)

    @pl.when(unit == 0)
    def _():
        dkv_sum[...] = jnp.zeros_like(dkv_sum)

    for head in range(heads):
        product = head_part(g_ref[0], head).astype(jnp.float32) * head_part(
            attn_ref[0], head
        ).astype(jnp.float32)
        delta[pl.ds(head, 1), :] = jnp.sum(product.T, 0, keepdims=True)

    def visit(block, diagonal):
        keys = kv_ref[block, :, :HEAD_SIZE]
        values = kv_ref[block, :, HEAD_SIZE:]
        key_sum, value_sum = None, None
        for head in range(heads):
            at = pl.ds(head, 1)
            queries = head_part(q_ref[0], head)
            grads = head_part(g_ref[0], head)
            scores = dot(keys, queries, CONTRACT_LAST)
            if diagonal:
                scores = diagonal_mask(scores)
            probs = jnp.exp2(scores * EXP2_SCALE - total_ref[0, at, :])
            grad_probs = dot(values, grads, CONTRACT_LAST)
            grad_scores = (probs * (grad_probs - delta[at, :])).astype(jnp.bfloat16)
            value_add = dot(probs.astype(jnp.bfloat16), grads)
            key_add = dot(grad_scores, queries)
            query_add = dot(keys, grad_scores, CONTRACT_FIRST)
            dq_sum[head] = query_add if diagonal else dq_sum[head] + query_add
            key_sum = key_add if head == 0 else key_sum + key_add
            value_sum = value_add if head == 0 else value_sum + value_add
        dkv_sum[block, :, :HEAD_SIZE] += key_sum * score_scale
        dkv_sum[block, :, HEAD_SIZE:] += value_sum

    visit(rows_ref[unit, 0], True)

    @pl.loop(1, rows_ref.shape[1])
    def _(slot):
        block = rows_ref[unit, slot]

        @pl.when(block >= 0)
        def _():
            visit(block, False)

    for head in range(heads):
        dq_ref[0, :, head * HEAD_SIZE : (head + 1) * HEAD_SIZE] = (
            (dq_sum[head] * score_scale).T.astype(dq_ref.dtype)
        )

    @pl.when(unit == pl.num_programs(0) - 1)
    def _():
        dkv_ref[...] = dkv_sum[...].astype(dkv_ref.dtype)


def backward_units(rows, q_units, g_units, attn_units, totals, kv_all):
    units, tokens, width = q_units.shape
    heads = width // HEAD_SIZE
    whole = pl.BlockSpec(kv_all.shape, lambda unit, rows: (0, 0, 0))
    per_unit = pl.BlockSpec((1, tokens, width), lambda unit, rows: (unit, 0, 0))
    per_total = pl.BlockSpec((1, heads, tokens), lambda unit, rows: (unit, 0, 0))
    return pl.pallas_call(
        backward_kernel,
        grid_spec=pltpu.PrefetchScalarGridSpec(
            num_scalar_prefetch=1,
            grid=(units,),
            in_specs=[per_unit, per_unit, per_unit, per_total, whole],
            out_specs=(per_unit, whole),
            scratch_shapes=[
                pltpu.VMEM((heads, tokens), jnp.float32),
                pltpu.VMEM((heads, HEAD_SIZE, tokens), jnp.float32),
                pltpu.VMEM(kv_all.shape, jnp.float32),
            ],
        ),
        out_shape=(
            jax.ShapeDtypeStruct(q_units.shape, jnp.bfloat16),
            jax.ShapeDtypeStruct(kv_all.shape, jnp.bfloat16),
        ),
        compiler_params=pltpu.CompilerParams(vmem_limit_bytes=VMEM_BYTES),
        cost_estimate=pl.CostEstimate(
            flops=50 * tokens * tokens * width,
            bytes_accessed=kv_all.size * 4,
            transcendentals=5 * tokens * tokens * heads,
        ),
    )(rows, q_units, g_units, attn_units, totals, kv_all)


def halves_of(value):
    half = value.shape[1] // 2
    return jnp.stack([value[:, :half], value[:, half:]])


def to_units(home, core, count):
    first, second = home[0], home[1]
    even = range(0, count, 2)
    one = lax.ppermute(
        jnp.where(core == 0, second, first),
        "ctx",
        [(c, c + 1) for c in even] + [(c + 1, count - 2 - c) for c in even],
    )
    two = lax.ppermute(second, "ctx", [(c + 1, count - 1 - c) for c in even])
    return jnp.stack([jnp.where(core == 0, first, one), jnp.where(core == 0, one, two)])


def to_home(units, core, count):
    even = range(0, count, 2)
    one = lax.ppermute(
        jnp.where(core == 0, units[1], units[0]),
        "ctx",
        [(c, count - 1 - c) for c in even] + [(c + 1, c) for c in even],
    )
    two = lax.ppermute(units[1], "ctx", [(c + 1, count - 1 - c) for c in even])
    return jnp.concatenate(
        [jnp.where(core == 0, units[0], one), jnp.where(core == 0, one, two)], 1
    )


def paired_device(query_proj, projected_keys, projected_values, w_out, attended_blocks, grad_out):
    count = lax.axis_size("ctx")
    me = lax.axis_index("ctx")
    core = lax.rem(me, 2)
    tokens = query_proj.shape[0]
    piece = lax.all_gather(grad_out, "head", axis=1, tiled=True)
    key_halves, value_halves = halves_of(projected_keys), halves_of(projected_values)
    kv_all, q_units = exchange(
        spread_kernel,
        0,
        count,
        jnp.concatenate([key_halves, value_halves], 2),
        halves_of(query_proj),
    )
    own_even = me - core
    rows = jnp.take(attended_blocks, jnp.stack([own_even, count - 1 - own_even]), axis=0)
    attn_units, totals = forward_units(rows, q_units, kv_all)
    attn = to_home(attn_units, core, count)
    out_terms = dot(attn, w_out)
    layer_out = lax.psum_scatter(
        out_terms.astype(jnp.bfloat16), "head", scatter_dimension=1, tiled=True
    )
    grad_attn = dot(piece, w_out, CONTRACT_LAST).astype(jnp.bfloat16)
    g_units = to_units(halves_of(grad_attn), core, count)
    weight_terms = dot(attn, piece, CONTRACT_FIRST)
    grad_wout = lax.psum_scatter(
        weight_terms.astype(jnp.bfloat16), "ctx", scatter_dimension=1, tiled=True
    ).astype(jnp.float32)
    dq_units, dkv = backward_units(rows, q_units, g_units, attn_units, totals, kv_all)
    dkv_all, dq_halves = exchange(return_kernel, 1, count, dkv, dq_units)
    grad_query = jnp.concatenate([dq_halves[0], dq_halves[1]], 1).astype(jnp.float32)
    summed = jnp.sum(
        dkv_all.reshape(count // 2, 2, tokens, 2 * HEAD_SIZE).astype(jnp.float32), 0
    )
    grad_key = jnp.concatenate([summed[0, :, :HEAD_SIZE], summed[1, :, :HEAD_SIZE]], 1)
    grad_value = jnp.concatenate([summed[0, :, HEAD_SIZE:], summed[1, :, HEAD_SIZE:]], 1)
    return (layer_out, grad_query, grad_key, grad_value, grad_wout)


def per_device(query_proj, projected_keys, projected_values, w_out, attended_blocks, grad_out):
    count = lax.axis_size("ctx")
    pairs = (
        projected_keys.shape[1] == 2 * HEAD_SIZE
        and query_proj.shape[0] == BLOCK_TOKENS
        and count % 4 == 0
        and attended_blocks.shape[1] >= count
    )
    body = paired_device if pairs else general_device
    return body(
        query_proj, projected_keys, projected_values, w_out, attended_blocks, grad_out
    )


def solution(mesh):
    return jax.shard_map(
        per_device,
        mesh=mesh,
        in_specs=(
            P("ctx", "head"),
            P("ctx", "head"),
            P("ctx", "head"),
            P("head", None),
            P(),
            P("ctx", "head"),
        ),
        out_specs=(
            P("ctx", "head"),
            P("ctx", "head"),
            P("ctx", "head"),
            P("ctx", "head"),
            P("head", "ctx"),
        ),
        check_vma=False,
    )
```

```python
import functools
import math

import jax
import jax.numpy as jnp
from jax import lax
from jax.experimental import pallas as pl
from jax.experimental.pallas import tpu as pltpu
from jax.sharding import PartitionSpec as P

HEAD_SIZE = 128
BLOCK_TOKENS = 512


def shifted(value, axis, steps):
    count = lax.axis_size(axis)
    leading, last = (max(0, -steps), min(count, count - steps))
    return lax.ppermute(value, axis, [(source, source + steps) for source in range(leading, last)])


def load_key_block(source, local_index, kv_heads):
    rows_per_block = lax.dynamic_slice_in_dim(source, local_index * BLOCK_TOKENS, BLOCK_TOKENS, 0)
    return rows_per_block.reshape(BLOCK_TOKENS, kv_heads, HEAD_SIZE)


def causal_scores(query_portion, key_row_slice, key_block_index, diagonal_block):
    raw_scores = jnp.einsum(
        "ikgd,jkd->kgij", query_portion, key_row_slice, preferred_element_type=jnp.float32
    ) * HEAD_SIZE ** (-0.5)
    row_pos = lax.broadcasted_iota(jnp.int32, (BLOCK_TOKENS, BLOCK_TOKENS), 0)
    col_pos = lax.broadcasted_iota(jnp.int32, (BLOCK_TOKENS, BLOCK_TOKENS), 1)
    allowed = (key_block_index < diagonal_block) | (col_pos <= row_pos)
    return jnp.where(allowed, raw_scores, -jnp.inf)


def general_device(query_proj, projected_keys, projected_values, w_out, attended_blocks, grad_out):
    ctx_rank = lax.axis_index("ctx")
    ctx_count = lax.axis_size("ctx")
    local_rows = query_proj.shape[0]
    blocks_here = local_rows // BLOCK_TOKENS
    kv_heads = projected_keys.shape[1] // HEAD_SIZE
    key_column_span = projected_keys.shape[1]
    head_cols = query_proj.shape[1]
    heads_per_group = head_cols // HEAD_SIZE // kv_heads
    slot_count = attended_blocks.shape[1]
    score_scale = HEAD_SIZE ** (-0.5)
    reach = min((slot_count - 1 + blocks_here - 1) // blocks_here, ctx_count - 1)
    margin_rows = reach * local_rows
    far_step = ctx_count // 2
    use_far = far_step > reach
    window_rows = margin_rows + local_rows
    front_rows = max(reach, far_step) * local_rows
    all_keys, all_values = (
        lax.all_gather(projected_keys, "ctx", axis=0, tiled=True),
        lax.all_gather(projected_values, "ctx", axis=0, tiled=True),
    )
    total_rows = all_keys.shape[0]

    def heads_of(source):
        return source.reshape(BLOCK_TOKENS, kv_heads, heads_per_group, HEAD_SIZE)

    local_block = 0
    diagonal_block = ctx_rank * blocks_here + local_block
    listed = lax.dynamic_index_in_dim(attended_blocks, diagonal_block, 0, keepdims=False)
    query_portion = heads_of(query_proj)

    def forward_visit(slot_num, running):
        key_block_index = listed[slot_num]

        def forward_live(present_block):
            running_largest, softmax_denominator, weighted_values = present_block
            score_matrix = causal_scores(
                query_portion,
                load_key_block(all_keys, key_block_index, kv_heads),
                key_block_index,
                diagonal_block,
            )
            new_largest = jnp.maximum(running_largest, jnp.max(score_matrix, -1))
            rescale = jnp.exp(running_largest - new_largest)
            attention_weights = jnp.exp(score_matrix - new_largest[..., None])
            softmax_denominator = softmax_denominator * rescale + jnp.sum(attention_weights, -1)
            value_row_slice = load_key_block(all_values, key_block_index, kv_heads)
            weighted_values = weighted_values * rescale[..., None] + jnp.einsum(
                "mayf,fmb->mayb",
                attention_weights.astype(jnp.bfloat16),
                value_row_slice,
                preferred_element_type=jnp.float32,
            )
            return (new_largest, softmax_denominator, weighted_values)

        return lax.cond(
            key_block_index >= 0, forward_live, lambda present_block: present_block, running
        )

    initial_state = (
        jnp.full((kv_heads, heads_per_group, BLOCK_TOKENS), -jnp.inf, jnp.float32),
        jnp.zeros((kv_heads, heads_per_group, BLOCK_TOKENS), jnp.float32),
        jnp.zeros((kv_heads, heads_per_group, BLOCK_TOKENS, HEAD_SIZE), jnp.float32),
    )
    running_largest, softmax_denominator, weighted_values = lax.fori_loop(
        0, slot_count, forward_visit, initial_state
    )
    attn_block = (weighted_values / softmax_denominator[..., None]).astype(jnp.bfloat16)
    attn_parts = attn_block.transpose(2, 0, 1, 3).reshape(BLOCK_TOKENS, head_cols)
    log_totals = [running_largest + jnp.log(softmax_denominator)]
    out_terms = jnp.dot(attn_parts, w_out, preferred_element_type=jnp.float32)
    layer_out = lax.psum_scatter(
        out_terms.astype(jnp.bfloat16), "head", scatter_dimension=1, tiled=True
    )
    piece = lax.all_gather(grad_out, "head", axis=1, tiled=True)
    grad_sum = lax.dot_general(
        piece, w_out, (((1,), (1,)), ((), ())), preferred_element_type=jnp.float32
    )
    column_term = lax.dot_general(
        attn_parts, piece, (((0,), (0,)), ((), ())), preferred_element_type=jnp.float32
    )
    weight_terms = column_term
    grad_sum, weight_terms = (grad_sum, weight_terms)
    grad_attn = grad_sum.astype(jnp.bfloat16)
    grad_wout = lax.psum_scatter(
        weight_terms.astype(jnp.bfloat16), "ctx", scatter_dimension=1, tiled=True
    ).astype(jnp.float32)
    key_gradient_totals = jnp.zeros((total_rows, key_column_span), jnp.float32)
    value_gradient_totals = jnp.zeros((total_rows, key_column_span), jnp.float32)
    local_block = 0
    diagonal_block = ctx_rank * blocks_here + local_block
    listed = lax.dynamic_index_in_dim(attended_blocks, diagonal_block, 0, keepdims=False)
    query_portion = heads_of(query_proj)
    grad_heads = heads_of(grad_attn)
    attn_heads = heads_of(attn_parts)
    delta = jnp.einsum("ikgd,ikgd->kgi", grad_heads, attn_heads, preferred_element_type=jnp.float32)
    log_total = log_totals[local_block]

    def reverse_visit(slot_num, running):
        key_block_index = listed[slot_num]

        def reverse_live(present_block):
            query_gradient_total, key_buffer, value_buffer = present_block
            key_row_slice = load_key_block(all_keys, key_block_index, kv_heads)
            value_row_slice = load_key_block(all_values, key_block_index, kv_heads)
            score_matrix = causal_scores(
                query_portion, key_row_slice, key_block_index, diagonal_block
            )
            probs = jnp.exp(score_matrix - log_total[..., None])
            grad_probs = jnp.einsum(
                "ikgd,jkd->kgij", grad_heads, value_row_slice, preferred_element_type=jnp.float32
            )
            grad_scores = (score_scale * probs * (grad_probs - delta[..., None])).astype(
                jnp.bfloat16
            )
            query_gradient_total = query_gradient_total + jnp.einsum(
                "mayf,fmb->mayb", grad_scores, key_row_slice, preferred_element_type=jnp.float32
            )
            key_add = jnp.einsum(
                "kgij,ikgd->jkd", grad_scores, query_portion, preferred_element_type=jnp.float32
            ).reshape(BLOCK_TOKENS, -1)
            value_add = jnp.einsum(
                "kgij,ikgd->jkd",
                probs.astype(jnp.bfloat16),
                grad_heads,
                preferred_element_type=jnp.float32,
            ).reshape(BLOCK_TOKENS, -1)
            begin = key_block_index * BLOCK_TOKENS
            key_buffer = lax.dynamic_update_slice_in_dim(
                key_buffer,
                lax.dynamic_slice_in_dim(key_buffer, begin, BLOCK_TOKENS, 0) + key_add,
                begin,
                0,
            )
            value_buffer = lax.dynamic_update_slice_in_dim(
                value_buffer,
                lax.dynamic_slice_in_dim(value_buffer, begin, BLOCK_TOKENS, 0) + value_add,
                begin,
                0,
            )
            return (query_gradient_total, key_buffer, value_buffer)

        return lax.cond(
            key_block_index >= 0, reverse_live, lambda present_block: present_block, running
        )

    initial_state = (
        jnp.zeros((kv_heads, heads_per_group, BLOCK_TOKENS, HEAD_SIZE), jnp.float32),
        key_gradient_totals,
        value_gradient_totals,
    )
    query_gradient_total, key_gradient_totals, value_gradient_totals = lax.fori_loop(
        0, slot_count, reverse_visit, initial_state
    )
    query_grads = query_gradient_total.transpose(2, 0, 1, 3).reshape(BLOCK_TOKENS, head_cols)

    def to_window(buffer):
        padded = jnp.concatenate([jnp.zeros((front_rows, key_column_span), jnp.float32), buffer], 0)
        window_part = lax.dynamic_slice_in_dim(
            padded, front_rows - margin_rows + ctx_rank * local_rows, window_rows, 0
        )
        if use_far:
            far_part = lax.dynamic_slice_in_dim(
                padded, front_rows + (ctx_rank - far_step) * local_rows, local_rows, 0
            )
            return jnp.concatenate([window_part, far_part], 0)
        return window_part

    low_keys = to_window(key_gradient_totals).astype(jnp.bfloat16)
    low_values = to_window(value_gradient_totals).astype(jnp.bfloat16)
    grad_key = low_keys[margin_rows:window_rows].astype(jnp.float32)
    grad_value = low_values[margin_rows:window_rows].astype(jnp.float32)
    for distance in range(1, reach + 1):
        begin = (reach - distance) * local_rows
        back_keys, back_values = shifted(
            (low_keys[begin : begin + local_rows], low_values[begin : begin + local_rows]),
            "ctx",
            -distance,
        )
        grad_key = grad_key + back_keys.astype(jnp.float32)
        grad_value = grad_value + back_values.astype(jnp.float32)
    if use_far:
        far_back_keys, far_back_values = shifted(
            (low_keys[window_rows:], low_values[window_rows:]), "ctx", -far_step
        )
        grad_key = grad_key + far_back_keys.astype(jnp.float32)
        grad_value = grad_value + far_back_values.astype(jnp.float32)
    return (layer_out, query_grads, grad_key, grad_value, grad_wout)


MESH = pl.DeviceIdType.MESH
VMEM_BYTES = 48 * 1024 * 1024
EXP2_SCALE = HEAD_SIZE ** (-0.5) * math.log2(math.e)
CONTRACT_LAST = (((1,), (1,)), ((), ()))
CONTRACT_FIRST = (((0,), (0,)), ((), ()))


def dot(left, right, dims=(((1,), (0,)), ((), ()))):
    return lax.dot_general(left, right, dims, preferred_element_type=jnp.float32)


def greet(peers, count):
    barrier = pltpu.get_barrier_semaphore()
    for peer in peers:
        pl.semaphore_signal(barrier, inc=1, device_id={"ctx": peer}, device_id_type=MESH)
    pl.semaphore_wait(barrier, count)


def remote(source, target, send_sem, recv_sem, peer):
    return pltpu.make_async_remote_copy(
        src_ref=source,
        dst_ref=target,
        send_sem=send_sem,
        recv_sem=recv_sem,
        device_id={"ctx": peer},
        device_id_type=MESH,
    )


def exchange_kernel(count, by_core, blocks_ref, halves_ref, blocks_all, other, send, recv, half, local):
    me = lax.axis_index("ctx")
    core = lax.rem(me, 2)
    greet([lax.rem(me + step, count) for step in range(1, count)], count - 1)
    source = halves_ref.at[1 - core] if by_core else halves_ref.at[1]
    copies = [remote(source, other, half.at[0], half.at[1], count - 1 - me)]
    copies[0].start()
    for step in range(1, count):
        peer = lax.rem(me + step, count)
        index = lax.rem(peer, 2) if by_core else peer
        copy = remote(blocks_ref.at[index], blocks_all.at[me], send.at[step], recv.at[step], peer)
        copy.start()
        copies.append(copy)
    index = core if by_core else me
    mine = pltpu.make_async_copy(blocks_ref.at[index], blocks_all.at[me], local)
    mine.start()
    mine.wait()
    for copy in copies:
        copy.wait()


def exchange(by_core, collective_id, count, blocks, units):
    any_space = pl.BlockSpec(memory_space=pl.ANY)
    return pl.pallas_call(
        functools.partial(exchange_kernel, count, by_core),
        out_shape=(
            jax.ShapeDtypeStruct((count,) + blocks.shape[1:], blocks.dtype),
            jax.ShapeDtypeStruct(units.shape[1:], units.dtype),
        ),
        in_specs=[any_space, any_space],
        out_specs=(any_space, any_space),
        scratch_shapes=[
            pltpu.SemaphoreType.DMA((count,)),
            pltpu.SemaphoreType.DMA((count,)),
            pltpu.SemaphoreType.DMA((2,)),
            pltpu.SemaphoreType.DMA,
        ],
        compiler_params=pltpu.CompilerParams(
            collective_id=collective_id, has_side_effects=True, vmem_limit_bytes=VMEM_BYTES
        ),
        cost_estimate=pl.CostEstimate(
            flops=0, bytes_accessed=2 * blocks.size * 2 + units.size * 4, transcendentals=0
        ),
    )(blocks, units)


def head_part(value, head):
    return value[:, head * HEAD_SIZE : (head + 1) * HEAD_SIZE]


def diagonal_mask(scores):
    key_row = lax.broadcasted_iota(jnp.int32, scores.shape, 0)
    query_col = lax.broadcasted_iota(jnp.int32, scores.shape, 1)
    return jnp.where(key_row <= query_col, scores, -jnp.inf)


def forward_kernel(rows_ref, q_ref, kv_ref, attn_ref, total_ref, largest, denominator, weighted):
    unit = pl.program_id(0)
    heads = q_ref.shape[2] // HEAD_SIZE

    def visit(block, diagonal):
        keys = kv_ref[block, :, :HEAD_SIZE]
        values = kv_ref[block, :, HEAD_SIZE:]
        for head in range(heads):
            at = pl.ds(head, 1)
            scores = dot(keys, head_part(q_ref[0], head), CONTRACT_LAST)
            if diagonal:
                scores = diagonal_mask(scores)
            top = jnp.max(scores, 0, keepdims=True)
            if not diagonal:
                before = largest[at, :]
                top = jnp.maximum(before, top)
                rescale = jnp.exp2((before - top) * EXP2_SCALE)
            weights = jnp.exp2(scores * EXP2_SCALE - top * EXP2_SCALE)
            added = jnp.sum(weights, 0, keepdims=True)
            product = dot(values, weights.astype(jnp.bfloat16), CONTRACT_FIRST)
            largest[at, :] = top
            if diagonal:
                denominator[at, :] = added
                weighted[head] = product
            else:
                denominator[at, :] = denominator[at, :] * rescale + added
                weighted[head] = weighted[head] * rescale + product

    visit(rows_ref[unit, 0], True)

    @pl.loop(1, rows_ref.shape[1])
    def _(slot):
        block = rows_ref[unit, slot]

        @pl.when(block >= 0)
        def _():
            visit(block, False)

    for head in range(heads):
        at = pl.ds(head, 1)
        bottom = denominator[at, :]
        attn_ref[0, :, head * HEAD_SIZE : (head + 1) * HEAD_SIZE] = (
            (weighted[head] / bottom).T.astype(jnp.bfloat16)
        )
        total_ref[0, at, :] = largest[at, :] * EXP2_SCALE + jnp.log2(bottom)


def forward_units(rows, q_units, kv_all):
    units, tokens, width = q_units.shape
    heads = width // HEAD_SIZE
    whole = pl.BlockSpec(kv_all.shape, lambda unit, rows: (0, 0, 0))
    per_unit = pl.BlockSpec((1, tokens, width), lambda unit, rows: (unit, 0, 0))
    per_total = pl.BlockSpec((1, heads, tokens), lambda unit, rows: (unit, 0, 0))
    return pl.pallas_call(
        forward_kernel,
        grid_spec=pltpu.PrefetchScalarGridSpec(
            num_scalar_prefetch=1,
            grid=(units,),
            in_specs=[per_unit, whole],
            out_specs=(per_unit, per_total),
            scratch_shapes=[
                pltpu.VMEM((heads, tokens), jnp.float32),
                pltpu.VMEM((heads, tokens), jnp.float32),
                pltpu.VMEM((heads, HEAD_SIZE, tokens), jnp.float32),
            ],
        ),
        out_shape=(
            jax.ShapeDtypeStruct(q_units.shape, jnp.bfloat16),
            jax.ShapeDtypeStruct((units, heads, tokens), jnp.float32),
        ),
        compiler_params=pltpu.CompilerParams(vmem_limit_bytes=VMEM_BYTES),
        cost_estimate=pl.CostEstimate(
            flops=20 * tokens * tokens * width,
            bytes_accessed=kv_all.size * 2,
            transcendentals=5 * tokens * tokens * heads,
        ),
    )(rows, q_units, kv_all)


def backward_kernel(
    rows_ref, q_ref, g_ref, attn_ref, total_ref, kv_ref, dq_ref, dkv_ref, delta, dq_sum, dkv_sum
):
    unit = pl.program_id(0)
    heads = q_ref.shape[2] // HEAD_SIZE
    score_scale = HEAD_SIZE ** (-0.5)

    @pl.when(unit == 0)
    def _():
        dkv_sum[...] = jnp.zeros_like(dkv_sum)

    for head in range(heads):
        product = head_part(g_ref[0], head).astype(jnp.float32) * head_part(
            attn_ref[0], head
        ).astype(jnp.float32)
        delta[pl.ds(head, 1), :] = jnp.sum(product.T, 0, keepdims=True)

    def visit(block, diagonal):
        keys = kv_ref[block, :, :HEAD_SIZE]
        values = kv_ref[block, :, HEAD_SIZE:]
        key_sum, value_sum = None, None
        for head in range(heads):
            at = pl.ds(head, 1)
            queries = head_part(q_ref[0], head)
            grads = head_part(g_ref[0], head)
            scores = dot(keys, queries, CONTRACT_LAST)
            if diagonal:
                scores = diagonal_mask(scores)
            probs = jnp.exp2(scores * EXP2_SCALE - total_ref[0, at, :])
            grad_probs = dot(values, grads, CONTRACT_LAST)
            grad_scores = (probs * (grad_probs - delta[at, :])).astype(jnp.bfloat16)
            value_add = dot(probs.astype(jnp.bfloat16), grads)
            key_add = dot(grad_scores, queries)
            query_add = dot(keys, grad_scores, CONTRACT_FIRST)
            dq_sum[head] = query_add if diagonal else dq_sum[head] + query_add
            key_sum = key_add if head == 0 else key_sum + key_add
            value_sum = value_add if head == 0 else value_sum + value_add
        dkv_sum[block, :, :HEAD_SIZE] += key_sum * score_scale
        dkv_sum[block, :, HEAD_SIZE:] += value_sum

    visit(rows_ref[unit, 0], True)

    @pl.loop(1, rows_ref.shape[1])
    def _(slot):
        block = rows_ref[unit, slot]

        @pl.when(block >= 0)
        def _():
            visit(block, False)

    for head in range(heads):
        dq_ref[0, :, head * HEAD_SIZE : (head + 1) * HEAD_SIZE] = (
            (dq_sum[head] * score_scale).T.astype(dq_ref.dtype)
        )

    @pl.when(unit == pl.num_programs(0) - 1)
    def _():
        dkv_ref[...] = dkv_sum[...].astype(dkv_ref.dtype)


def backward_units(rows, q_units, g_units, attn_units, totals, kv_all):
    units, tokens, width = q_units.shape
    heads = width // HEAD_SIZE
    whole = pl.BlockSpec(kv_all.shape, lambda unit, rows: (0, 0, 0))
    per_unit = pl.BlockSpec((1, tokens, width), lambda unit, rows: (unit, 0, 0))
    per_total = pl.BlockSpec((1, heads, tokens), lambda unit, rows: (unit, 0, 0))
    return pl.pallas_call(
        backward_kernel,
        grid_spec=pltpu.PrefetchScalarGridSpec(
            num_scalar_prefetch=1,
            grid=(units,),
            in_specs=[per_unit, per_unit, per_unit, per_total, whole],
            out_specs=(per_unit, whole),
            scratch_shapes=[
                pltpu.VMEM((heads, tokens), jnp.float32),
                pltpu.VMEM((heads, HEAD_SIZE, tokens), jnp.float32),
                pltpu.VMEM(kv_all.shape, jnp.float32),
            ],
        ),
        out_shape=(
            jax.ShapeDtypeStruct(q_units.shape, jnp.bfloat16),
            jax.ShapeDtypeStruct(kv_all.shape, jnp.bfloat16),
        ),
        compiler_params=pltpu.CompilerParams(vmem_limit_bytes=VMEM_BYTES),
        cost_estimate=pl.CostEstimate(
            flops=50 * tokens * tokens * width,
            bytes_accessed=kv_all.size * 4,
            transcendentals=5 * tokens * tokens * heads,
        ),
    )(rows, q_units, g_units, attn_units, totals, kv_all)


def halves_of(value):
    half = value.shape[1] // 2
    return jnp.stack([value[:, :half], value[:, half:]])


def swapped(value, count):
    return lax.ppermute(value, "ctx", [(c, count - 1 - c) for c in range(count)])


def merged_cores(terms, core, count):
    tiles = terms.reshape(count // 2, 2, terms.shape[0] // count, terms.shape[1])
    kept = jnp.where(core == 0, tiles[:, 0], tiles[:, 1])
    given = jnp.where(core == 0, tiles[:, 1], tiles[:, 0])
    taken = lax.ppermute(given, "ctx", [(c, c ^ 1) for c in range(count)])
    return (kept.astype(jnp.float32) + taken.astype(jnp.float32)).astype(jnp.bfloat16)


def paired_device(query_proj, projected_keys, projected_values, w_out, attended_blocks, grad_out):
    count = lax.axis_size("ctx")
    me = lax.axis_index("ctx")
    core, chip = lax.rem(me, 2), lax.div(me, 2)
    tokens = query_proj.shape[0]
    piece = lax.all_gather(grad_out, "head", axis=1, tiled=True)
    key_halves, value_halves = halves_of(projected_keys), halves_of(projected_values)

    def own_half(halves):
        return jnp.where(core == 0, halves[0], halves[1])

    def both_halves(own, other):
        return jnp.concatenate(
            [jnp.where(core == 0, own, other), jnp.where(core == 0, other, own)], 1
        )

    query_halves = halves_of(query_proj)
    kv_all, q_other = exchange(
        True, 0, count, jnp.concatenate([key_halves, value_halves], 2), query_halves
    )
    q_units = jnp.stack([own_half(query_halves), q_other])
    rows = jnp.take(attended_blocks, jnp.stack([me, count - 1 - me]), axis=0)
    attn_units, totals = forward_units(rows, q_units, kv_all)
    attn = both_halves(attn_units[0], swapped(attn_units[1], count))
    out_terms = dot(attn, w_out).astype(jnp.bfloat16)
    piece, out_terms = lax.optimization_barrier((piece, out_terms))
    layer_out = lax.psum_scatter(out_terms, "head", scatter_dimension=1, tiled=True)
    merged = merged_cores(dot(piece, attn, CONTRACT_FIRST).astype(jnp.bfloat16), core, count)
    grad_halves = halves_of(dot(piece, w_out, CONTRACT_LAST).astype(jnp.bfloat16))
    grad_other = swapped(own_half(grad_halves[::-1]), count)
    g_units = jnp.stack([own_half(grad_halves), grad_other])
    merged, g_units = lax.optimization_barrier((merged, g_units))
    parts = []
    for turn in range(1, count // 2):
        part = lax.dynamic_index_in_dim(merged, chip ^ turn, 0, keepdims=False)
        parts.append(lax.ppermute(part, "ctx", [(c, c ^ (2 * turn)) for c in range(count)]))
    dq_units, dkv = backward_units(rows, q_units, g_units, attn_units, totals, kv_all)
    parts, dq_units, dkv = lax.optimization_barrier((parts, dq_units, dkv))
    dkv_all, dq_other = exchange(False, 1, count, dkv, dq_units)
    total = lax.dynamic_index_in_dim(merged, chip, 0, keepdims=False).astype(jnp.float32)
    for part in parts:
        total = total + part.astype(jnp.float32)
    grad_wout = total.T
    grad_query = both_halves(dq_units[0], dq_other).astype(jnp.float32)
    summed = jnp.sum(
        dkv_all.reshape(count // 2, 2, tokens, 2 * HEAD_SIZE).astype(jnp.float32), 0
    )
    grad_key = jnp.concatenate([summed[0, :, :HEAD_SIZE], summed[1, :, :HEAD_SIZE]], 1)
    grad_value = jnp.concatenate([summed[0, :, HEAD_SIZE:], summed[1, :, HEAD_SIZE:]], 1)
    return (layer_out, grad_query, grad_key, grad_value, grad_wout)


def per_device(query_proj, projected_keys, projected_values, w_out, attended_blocks, grad_out):
    count = lax.axis_size("ctx")
    pairs = (
        projected_keys.shape[1] == 2 * HEAD_SIZE
        and query_proj.shape[0] == BLOCK_TOKENS
        and count >= 4
        and count & (count - 1) == 0
        and attended_blocks.shape[1] >= count
    )
    body = paired_device if pairs else general_device
    return body(
        query_proj, projected_keys, projected_values, w_out, attended_blocks, grad_out
    )


def solution(mesh):
    return jax.shard_map(
        per_device,
        mesh=mesh,
        in_specs=(
            P("ctx", "head"),
            P("ctx", "head"),
            P("ctx", "head"),
            P("head", None),
            P(),
            P("ctx", "head"),
        ),
        out_specs=(
            P("ctx", "head"),
            P("ctx", "head"),
            P("ctx", "head"),
            P("ctx", "head"),
            P("head", "ctx"),
        ),
        check_vma=False,
    )
```

```python
import functools
import math

import jax
import jax.numpy as jnp
from jax import lax
from jax.experimental import pallas as pl
from jax.experimental.pallas import tpu as pltpu
from jax.sharding import PartitionSpec as P

HEAD_SIZE = 128
BLOCK_TOKENS = 512


def shifted(value, axis, steps):
    count = lax.axis_size(axis)
    leading, last = (max(0, -steps), min(count, count - steps))
    return lax.ppermute(value, axis, [(source, source + steps) for source in range(leading, last)])


def load_key_block(source, local_index, kv_heads):
    rows_per_block = lax.dynamic_slice_in_dim(source, local_index * BLOCK_TOKENS, BLOCK_TOKENS, 0)
    return rows_per_block.reshape(BLOCK_TOKENS, kv_heads, HEAD_SIZE)


def causal_scores(query_portion, key_row_slice, key_block_index, diagonal_block):
    raw_scores = jnp.einsum(
        "ikgd,jkd->kgij", query_portion, key_row_slice, preferred_element_type=jnp.float32
    ) * HEAD_SIZE ** (-0.5)
    row_pos = lax.broadcasted_iota(jnp.int32, (BLOCK_TOKENS, BLOCK_TOKENS), 0)
    col_pos = lax.broadcasted_iota(jnp.int32, (BLOCK_TOKENS, BLOCK_TOKENS), 1)
    allowed = (key_block_index < diagonal_block) | (col_pos <= row_pos)
    return jnp.where(allowed, raw_scores, -jnp.inf)


def general_device(query_proj, projected_keys, projected_values, w_out, attended_blocks, grad_out):
    ctx_rank = lax.axis_index("ctx")
    ctx_count = lax.axis_size("ctx")
    local_rows = query_proj.shape[0]
    blocks_here = local_rows // BLOCK_TOKENS
    kv_heads = projected_keys.shape[1] // HEAD_SIZE
    key_column_span = projected_keys.shape[1]
    head_cols = query_proj.shape[1]
    heads_per_group = head_cols // HEAD_SIZE // kv_heads
    slot_count = attended_blocks.shape[1]
    score_scale = HEAD_SIZE ** (-0.5)
    reach = min((slot_count - 1 + blocks_here - 1) // blocks_here, ctx_count - 1)
    margin_rows = reach * local_rows
    far_step = ctx_count // 2
    use_far = far_step > reach
    window_rows = margin_rows + local_rows
    front_rows = max(reach, far_step) * local_rows
    all_keys, all_values = (
        lax.all_gather(projected_keys, "ctx", axis=0, tiled=True),
        lax.all_gather(projected_values, "ctx", axis=0, tiled=True),
    )
    total_rows = all_keys.shape[0]

    def heads_of(source):
        return source.reshape(BLOCK_TOKENS, kv_heads, heads_per_group, HEAD_SIZE)

    local_block = 0
    diagonal_block = ctx_rank * blocks_here + local_block
    listed = lax.dynamic_index_in_dim(attended_blocks, diagonal_block, 0, keepdims=False)
    query_portion = heads_of(query_proj)

    def forward_visit(slot_num, running):
        key_block_index = listed[slot_num]

        def forward_live(present_block):
            running_largest, softmax_denominator, weighted_values = present_block
            score_matrix = causal_scores(
                query_portion,
                load_key_block(all_keys, key_block_index, kv_heads),
                key_block_index,
                diagonal_block,
            )
            new_largest = jnp.maximum(running_largest, jnp.max(score_matrix, -1))
            rescale = jnp.exp(running_largest - new_largest)
            attention_weights = jnp.exp(score_matrix - new_largest[..., None])
            softmax_denominator = softmax_denominator * rescale + jnp.sum(attention_weights, -1)
            value_row_slice = load_key_block(all_values, key_block_index, kv_heads)
            weighted_values = weighted_values * rescale[..., None] + jnp.einsum(
                "mayf,fmb->mayb",
                attention_weights.astype(jnp.bfloat16),
                value_row_slice,
                preferred_element_type=jnp.float32,
            )
            return (new_largest, softmax_denominator, weighted_values)

        return lax.cond(
            key_block_index >= 0, forward_live, lambda present_block: present_block, running
        )

    initial_state = (
        jnp.full((kv_heads, heads_per_group, BLOCK_TOKENS), -jnp.inf, jnp.float32),
        jnp.zeros((kv_heads, heads_per_group, BLOCK_TOKENS), jnp.float32),
        jnp.zeros((kv_heads, heads_per_group, BLOCK_TOKENS, HEAD_SIZE), jnp.float32),
    )
    running_largest, softmax_denominator, weighted_values = lax.fori_loop(
        0, slot_count, forward_visit, initial_state
    )
    attn_block = (weighted_values / softmax_denominator[..., None]).astype(jnp.bfloat16)
    attn_parts = attn_block.transpose(2, 0, 1, 3).reshape(BLOCK_TOKENS, head_cols)
    log_totals = [running_largest + jnp.log(softmax_denominator)]
    out_terms = jnp.dot(attn_parts, w_out, preferred_element_type=jnp.float32)
    layer_out = lax.psum_scatter(
        out_terms.astype(jnp.bfloat16), "head", scatter_dimension=1, tiled=True
    )
    piece = lax.all_gather(grad_out, "head", axis=1, tiled=True)
    grad_sum = lax.dot_general(
        piece, w_out, (((1,), (1,)), ((), ())), preferred_element_type=jnp.float32
    )
    column_term = lax.dot_general(
        attn_parts, piece, (((0,), (0,)), ((), ())), preferred_element_type=jnp.float32
    )
    weight_terms = column_term
    grad_sum, weight_terms = (grad_sum, weight_terms)
    grad_attn = grad_sum.astype(jnp.bfloat16)
    grad_wout = lax.psum_scatter(
        weight_terms.astype(jnp.bfloat16), "ctx", scatter_dimension=1, tiled=True
    ).astype(jnp.float32)
    key_gradient_totals = jnp.zeros((total_rows, key_column_span), jnp.float32)
    value_gradient_totals = jnp.zeros((total_rows, key_column_span), jnp.float32)
    local_block = 0
    diagonal_block = ctx_rank * blocks_here + local_block
    listed = lax.dynamic_index_in_dim(attended_blocks, diagonal_block, 0, keepdims=False)
    query_portion = heads_of(query_proj)
    grad_heads = heads_of(grad_attn)
    attn_heads = heads_of(attn_parts)
    delta = jnp.einsum("ikgd,ikgd->kgi", grad_heads, attn_heads, preferred_element_type=jnp.float32)
    log_total = log_totals[local_block]

    def reverse_visit(slot_num, running):
        key_block_index = listed[slot_num]

        def reverse_live(present_block):
            query_gradient_total, key_buffer, value_buffer = present_block
            key_row_slice = load_key_block(all_keys, key_block_index, kv_heads)
            value_row_slice = load_key_block(all_values, key_block_index, kv_heads)
            score_matrix = causal_scores(
                query_portion, key_row_slice, key_block_index, diagonal_block
            )
            probs = jnp.exp(score_matrix - log_total[..., None])
            grad_probs = jnp.einsum(
                "ikgd,jkd->kgij", grad_heads, value_row_slice, preferred_element_type=jnp.float32
            )
            grad_scores = (score_scale * probs * (grad_probs - delta[..., None])).astype(
                jnp.bfloat16
            )
            query_gradient_total = query_gradient_total + jnp.einsum(
                "mayf,fmb->mayb", grad_scores, key_row_slice, preferred_element_type=jnp.float32
            )
            key_add = jnp.einsum(
                "kgij,ikgd->jkd", grad_scores, query_portion, preferred_element_type=jnp.float32
            ).reshape(BLOCK_TOKENS, -1)
            value_add = jnp.einsum(
                "kgij,ikgd->jkd",
                probs.astype(jnp.bfloat16),
                grad_heads,
                preferred_element_type=jnp.float32,
            ).reshape(BLOCK_TOKENS, -1)
            begin = key_block_index * BLOCK_TOKENS
            key_buffer = lax.dynamic_update_slice_in_dim(
                key_buffer,
                lax.dynamic_slice_in_dim(key_buffer, begin, BLOCK_TOKENS, 0) + key_add,
                begin,
                0,
            )
            value_buffer = lax.dynamic_update_slice_in_dim(
                value_buffer,
                lax.dynamic_slice_in_dim(value_buffer, begin, BLOCK_TOKENS, 0) + value_add,
                begin,
                0,
            )
            return (query_gradient_total, key_buffer, value_buffer)

        return lax.cond(
            key_block_index >= 0, reverse_live, lambda present_block: present_block, running
        )

    initial_state = (
        jnp.zeros((kv_heads, heads_per_group, BLOCK_TOKENS, HEAD_SIZE), jnp.float32),
        key_gradient_totals,
        value_gradient_totals,
    )
    query_gradient_total, key_gradient_totals, value_gradient_totals = lax.fori_loop(
        0, slot_count, reverse_visit, initial_state
    )
    query_grads = query_gradient_total.transpose(2, 0, 1, 3).reshape(BLOCK_TOKENS, head_cols)

    def to_window(buffer):
        padded = jnp.concatenate([jnp.zeros((front_rows, key_column_span), jnp.float32), buffer], 0)
        window_part = lax.dynamic_slice_in_dim(
            padded, front_rows - margin_rows + ctx_rank * local_rows, window_rows, 0
        )
        if use_far:
            far_part = lax.dynamic_slice_in_dim(
                padded, front_rows + (ctx_rank - far_step) * local_rows, local_rows, 0
            )
            return jnp.concatenate([window_part, far_part], 0)
        return window_part

    low_keys = to_window(key_gradient_totals).astype(jnp.bfloat16)
    low_values = to_window(value_gradient_totals).astype(jnp.bfloat16)
    grad_key = low_keys[margin_rows:window_rows].astype(jnp.float32)
    grad_value = low_values[margin_rows:window_rows].astype(jnp.float32)
    for distance in range(1, reach + 1):
        begin = (reach - distance) * local_rows
        back_keys, back_values = shifted(
            (low_keys[begin : begin + local_rows], low_values[begin : begin + local_rows]),
            "ctx",
            -distance,
        )
        grad_key = grad_key + back_keys.astype(jnp.float32)
        grad_value = grad_value + back_values.astype(jnp.float32)
    if use_far:
        far_back_keys, far_back_values = shifted(
            (low_keys[window_rows:], low_values[window_rows:]), "ctx", -far_step
        )
        grad_key = grad_key + far_back_keys.astype(jnp.float32)
        grad_value = grad_value + far_back_values.astype(jnp.float32)
    return (layer_out, query_grads, grad_key, grad_value, grad_wout)


MESH = pl.DeviceIdType.MESH
VMEM_BYTES = 48 * 1024 * 1024
EXP2_SCALE = HEAD_SIZE ** (-0.5) * math.log2(math.e)
CONTRACT_LAST = (((1,), (1,)), ((), ()))
CONTRACT_FIRST = (((0,), (0,)), ((), ()))


def dot(left, right, dims=(((1,), (0,)), ((), ()))):
    return lax.dot_general(left, right, dims, preferred_element_type=jnp.float32)


def greet(peers, count):
    barrier = pltpu.get_barrier_semaphore()
    for peer in peers:
        pl.semaphore_signal(barrier, inc=1, device_id={"ctx": peer}, device_id_type=MESH)
    pl.semaphore_wait(barrier, count)


def remote(source, target, send_sem, recv_sem, peer):
    return pltpu.make_async_remote_copy(
        src_ref=source,
        dst_ref=target,
        send_sem=send_sem,
        recv_sem=recv_sem,
        device_id={"ctx": peer},
        device_id_type=MESH,
    )


def exchange_kernel(count, by_core, blocks_ref, halves_ref, blocks_all, other, send, recv, half, local):
    me = lax.axis_index("ctx")
    core = lax.rem(me, 2)
    greet([lax.rem(me + step, count) for step in range(1, count)], count - 1)
    source = halves_ref.at[1 - core] if by_core else halves_ref.at[1]
    copies = [remote(source, other, half.at[0], half.at[1], count - 1 - me)]
    copies[0].start()
    for step in range(1, count):
        peer = lax.rem(me + step, count)
        index = lax.rem(peer, 2) if by_core else peer
        copy = remote(blocks_ref.at[index], blocks_all.at[me], send.at[step], recv.at[step], peer)
        copy.start()
        copies.append(copy)
    index = core if by_core else me
    mine = pltpu.make_async_copy(blocks_ref.at[index], blocks_all.at[me], local)
    mine.start()
    mine.wait()
    for copy in copies:
        copy.wait()


def exchange(by_core, collective_id, count, blocks, units):
    any_space = pl.BlockSpec(memory_space=pl.ANY)
    return pl.pallas_call(
        functools.partial(exchange_kernel, count, by_core),
        out_shape=(
            jax.ShapeDtypeStruct((count,) + blocks.shape[1:], blocks.dtype),
            jax.ShapeDtypeStruct(units.shape[1:], units.dtype),
        ),
        in_specs=[any_space, any_space],
        out_specs=(any_space, any_space),
        scratch_shapes=[
            pltpu.SemaphoreType.DMA((count,)),
            pltpu.SemaphoreType.DMA((count,)),
            pltpu.SemaphoreType.DMA((2,)),
            pltpu.SemaphoreType.DMA,
        ],
        compiler_params=pltpu.CompilerParams(
            collective_id=collective_id, has_side_effects=True, vmem_limit_bytes=VMEM_BYTES
        ),
        cost_estimate=pl.CostEstimate(
            flops=0, bytes_accessed=2 * blocks.size * 2 + units.size * 4, transcendentals=0
        ),
    )(blocks, units)


def head_part(value, head):
    return value[:, head * HEAD_SIZE : (head + 1) * HEAD_SIZE]


def diagonal_mask(scores):
    key_row = lax.broadcasted_iota(jnp.int32, scores.shape, 0)
    query_col = lax.broadcasted_iota(jnp.int32, scores.shape, 1)
    return jnp.where(key_row <= query_col, scores, -jnp.inf)


def forward_kernel(rows_ref, q_ref, kv_ref, attn_ref, total_ref, largest, denominator, weighted):
    unit = pl.program_id(0)
    heads = q_ref.shape[2] // HEAD_SIZE

    def visit(block, diagonal):
        keys = kv_ref[block, :, :HEAD_SIZE]
        values = kv_ref[block, :, HEAD_SIZE:]
        for head in range(heads):
            at = pl.ds(head, 1)
            scores = dot(keys, head_part(q_ref[0], head), CONTRACT_LAST)
            if diagonal:
                scores = diagonal_mask(scores)
            top = jnp.max(scores, 0, keepdims=True)
            if not diagonal:
                before = largest[at, :]
                top = jnp.maximum(before, top)
                rescale = jnp.exp2((before - top) * EXP2_SCALE)
            weights = jnp.exp2(scores * EXP2_SCALE - top * EXP2_SCALE)
            added = jnp.sum(weights, 0, keepdims=True)
            product = dot(values, weights.astype(jnp.bfloat16), CONTRACT_FIRST)
            largest[at, :] = top
            if diagonal:
                denominator[at, :] = added
                weighted[head] = product
            else:
                denominator[at, :] = denominator[at, :] * rescale + added
                weighted[head] = weighted[head] * rescale + product

    visit(rows_ref[unit, 0], True)

    @pl.loop(1, rows_ref.shape[1])
    def _(slot):
        block = rows_ref[unit, slot]

        @pl.when(block >= 0)
        def _():
            visit(block, False)

    for head in range(heads):
        at = pl.ds(head, 1)
        bottom = denominator[at, :]
        attn_ref[0, :, head * HEAD_SIZE : (head + 1) * HEAD_SIZE] = (
            (weighted[head] / bottom).T.astype(jnp.bfloat16)
        )
        total_ref[0, at, :] = largest[at, :] * EXP2_SCALE + jnp.log2(bottom)


def forward_units(rows, q_units, kv_all):
    units, tokens, width = q_units.shape
    heads = width // HEAD_SIZE
    whole = pl.BlockSpec(kv_all.shape, lambda unit, rows: (0, 0, 0))
    per_unit = pl.BlockSpec((1, tokens, width), lambda unit, rows: (unit, 0, 0))
    per_total = pl.BlockSpec((1, heads, tokens), lambda unit, rows: (unit, 0, 0))
    return pl.pallas_call(
        forward_kernel,
        grid_spec=pltpu.PrefetchScalarGridSpec(
            num_scalar_prefetch=1,
            grid=(units,),
            in_specs=[per_unit, whole],
            out_specs=(per_unit, per_total),
            scratch_shapes=[
                pltpu.VMEM((heads, tokens), jnp.float32),
                pltpu.VMEM((heads, tokens), jnp.float32),
                pltpu.VMEM((heads, HEAD_SIZE, tokens), jnp.float32),
            ],
        ),
        out_shape=(
            jax.ShapeDtypeStruct(q_units.shape, jnp.bfloat16),
            jax.ShapeDtypeStruct((units, heads, tokens), jnp.float32),
        ),
        compiler_params=pltpu.CompilerParams(vmem_limit_bytes=VMEM_BYTES),
        cost_estimate=pl.CostEstimate(
            flops=20 * tokens * tokens * width,
            bytes_accessed=kv_all.size * 2,
            transcendentals=5 * tokens * tokens * heads,
        ),
    )(rows, q_units, kv_all)


def backward_kernel(
    rows_ref, q_ref, g_ref, attn_ref, total_ref, kv_ref, dq_ref, dkv_ref, delta, dq_sum, dkv_sum
):
    unit = pl.program_id(0)
    heads = q_ref.shape[2] // HEAD_SIZE
    score_scale = HEAD_SIZE ** (-0.5)

    @pl.when(unit == 0)
    def _():
        dkv_sum[...] = jnp.zeros_like(dkv_sum)

    for head in range(heads):
        product = head_part(g_ref[0], head).astype(jnp.float32) * head_part(
            attn_ref[0], head
        ).astype(jnp.float32)
        delta[pl.ds(head, 1), :] = jnp.sum(product.T, 0, keepdims=True)

    def visit(block, diagonal):
        keys = kv_ref[block, :, :HEAD_SIZE]
        values = kv_ref[block, :, HEAD_SIZE:]
        key_sum, value_sum = None, None
        for head in range(heads):
            at = pl.ds(head, 1)
            queries = head_part(q_ref[0], head)
            grads = head_part(g_ref[0], head)
            scores = dot(keys, queries, CONTRACT_LAST)
            if diagonal:
                scores = diagonal_mask(scores)
            probs = jnp.exp2(scores * EXP2_SCALE - total_ref[0, at, :])
            grad_probs = dot(values, grads, CONTRACT_LAST)
            grad_scores = (probs * (grad_probs - delta[at, :])).astype(jnp.bfloat16)
            value_add = dot(probs.astype(jnp.bfloat16), grads)
            key_add = dot(grad_scores, queries)
            query_add = dot(keys, grad_scores, CONTRACT_FIRST)
            dq_sum[head] = query_add if diagonal else dq_sum[head] + query_add
            key_sum = key_add if head == 0 else key_sum + key_add
            value_sum = value_add if head == 0 else value_sum + value_add
        dkv_sum[block, :, :HEAD_SIZE] += key_sum * score_scale
        dkv_sum[block, :, HEAD_SIZE:] += value_sum

    visit(rows_ref[unit, 0], True)

    @pl.loop(1, rows_ref.shape[1])
    def _(slot):
        block = rows_ref[unit, slot]

        @pl.when(block >= 0)
        def _():
            visit(block, False)

    for head in range(heads):
        dq_ref[0, :, head * HEAD_SIZE : (head + 1) * HEAD_SIZE] = (
            (dq_sum[head] * score_scale).T.astype(dq_ref.dtype)
        )

    @pl.when(unit == pl.num_programs(0) - 1)
    def _():
        dkv_ref[...] = dkv_sum[...].astype(dkv_ref.dtype)


def backward_units(rows, q_units, g_units, attn_units, totals, kv_all):
    units, tokens, width = q_units.shape
    heads = width // HEAD_SIZE
    whole = pl.BlockSpec(kv_all.shape, lambda unit, rows: (0, 0, 0))
    per_unit = pl.BlockSpec((1, tokens, width), lambda unit, rows: (unit, 0, 0))
    per_total = pl.BlockSpec((1, heads, tokens), lambda unit, rows: (unit, 0, 0))
    return pl.pallas_call(
        backward_kernel,
        grid_spec=pltpu.PrefetchScalarGridSpec(
            num_scalar_prefetch=1,
            grid=(units,),
            in_specs=[per_unit, per_unit, per_unit, per_total, whole],
            out_specs=(per_unit, whole),
            scratch_shapes=[
                pltpu.VMEM((heads, tokens), jnp.float32),
                pltpu.VMEM((heads, HEAD_SIZE, tokens), jnp.float32),
                pltpu.VMEM(kv_all.shape, jnp.float32),
            ],
        ),
        out_shape=(
            jax.ShapeDtypeStruct(q_units.shape, jnp.bfloat16),
            jax.ShapeDtypeStruct(kv_all.shape, jnp.bfloat16),
        ),
        compiler_params=pltpu.CompilerParams(vmem_limit_bytes=VMEM_BYTES),
        cost_estimate=pl.CostEstimate(
            flops=50 * tokens * tokens * width,
            bytes_accessed=kv_all.size * 4,
            transcendentals=5 * tokens * tokens * heads,
        ),
    )(rows, q_units, g_units, attn_units, totals, kv_all)


def halves_of(value):
    half = value.shape[1] // 2
    return jnp.stack([value[:, :half], value[:, half:]])


def swapped(value, count):
    return lax.ppermute(value, "ctx", [(c, count - 1 - c) for c in range(count)])


def merged_cores(terms, core, count):
    tiles = terms.reshape(count // 2, 2, terms.shape[0] // count, terms.shape[1])
    kept = jnp.where(core == 0, tiles[:, 0], tiles[:, 1])
    given = jnp.where(core == 0, tiles[:, 1], tiles[:, 0])
    taken = lax.ppermute(given, "ctx", [(c, c ^ 1) for c in range(count)])
    return (kept.astype(jnp.float32) + taken.astype(jnp.float32)).astype(jnp.bfloat16)


def chip_parts(merged, chip, count):
    parts = []
    for turn in range(1, count // 2):
        part = lax.dynamic_index_in_dim(merged, chip ^ turn, 0, keepdims=False)
        parts.append(lax.ppermute(part, "ctx", [(c, c ^ (2 * turn)) for c in range(count)]))
    return parts


def sum_kernel(*refs):
    out_ref = refs[-1]
    width = refs[0].shape[0]
    per_chunk = (len(refs) - 1) // (out_ref.shape[1] // width)
    for chunk in range(out_ref.shape[1] // width):
        total = refs[chunk * per_chunk][...].astype(jnp.float32)
        for ref in refs[chunk * per_chunk + 1 : (chunk + 1) * per_chunk]:
            total += ref[...].astype(jnp.float32)
        out_ref[:, chunk * width : (chunk + 1) * width] = total.T


def summed_chunks(chunks):
    width, rows = chunks[0][0].shape
    flat = [term for chunk in chunks for term in chunk]
    return pl.pallas_call(
        sum_kernel,
        out_shape=jax.ShapeDtypeStruct((rows, width * len(chunks)), jnp.float32),
        compiler_params=pltpu.CompilerParams(vmem_limit_bytes=VMEM_BYTES),
    )(*flat)


def column_chunk(value, tiles, chunk):
    width = value.shape[1] // tiles // 2
    starts = [(2 * tile + chunk) * width for tile in range(tiles)]
    return jnp.concatenate([value[:, start : start + width] for start in starts], 1)


def paired_device(query_proj, projected_keys, projected_values, w_out, attended_blocks, grad_out):
    count, groups = lax.axis_size("ctx"), lax.axis_size("head")
    me = lax.axis_index("ctx")
    core, chip = lax.rem(me, 2), lax.div(me, 2)
    tokens = query_proj.shape[0]
    own_tiles = count // groups
    pieces = [
        lax.all_gather(column_chunk(grad_out, own_tiles, chunk), "head", axis=1, tiled=True)
        for chunk in range(2)
    ]
    key_halves, value_halves = halves_of(projected_keys), halves_of(projected_values)

    def own_half(halves):
        return jnp.where(core == 0, halves[0], halves[1])

    def both_halves(own, other):
        return jnp.concatenate(
            [jnp.where(core == 0, own, other), jnp.where(core == 0, other, own)], 1
        )

    def weight_terms(piece, attn):
        terms = dot(piece, attn, CONTRACT_FIRST).astype(jnp.bfloat16)
        return merged_cores(terms, core, count)

    query_halves = halves_of(query_proj)
    kv_all, q_other = exchange(
        True, 0, count, jnp.concatenate([key_halves, value_halves], 2), query_halves
    )
    weights = [column_chunk(w_out, count, chunk) for chunk in range(2)]
    q_units = jnp.stack([own_half(query_halves), q_other])
    rows = jnp.take(attended_blocks, jnp.stack([me, count - 1 - me]), axis=0)
    attn_units, totals = forward_units(rows, q_units, kv_all)
    attn = both_halves(attn_units[0], swapped(attn_units[1], count))
    out_terms = dot(attn, w_out).astype(jnp.bfloat16)
    first_merged = weight_terms(pieces[0], attn)
    first_grad = dot(pieces[0], weights[0], CONTRACT_LAST)
    first_parts = chip_parts(first_merged, chip, count)
    last_piece, out_terms, first_parts, first_grad = lax.optimization_barrier(
        (pieces[1], out_terms, first_parts, first_grad)
    )
    layer_out = lax.psum_scatter(out_terms, "head", scatter_dimension=1, tiled=True)
    grad_attn = first_grad + dot(last_piece, weights[1], CONTRACT_LAST)
    grad_halves = halves_of(grad_attn.astype(jnp.bfloat16))
    grad_other = swapped(own_half(grad_halves[::-1]), count)
    g_units = jnp.stack([own_half(grad_halves), grad_other])
    last_merged = weight_terms(last_piece, attn)
    last_merged, g_units = lax.optimization_barrier((last_merged, g_units))
    last_parts = chip_parts(last_merged, chip, count)
    dq_units, dkv = backward_units(rows, q_units, g_units, attn_units, totals, kv_all)
    last_parts, dq_units, dkv = lax.optimization_barrier((last_parts, dq_units, dkv))
    dkv_all, dq_other = exchange(False, 1, count, dkv, dq_units)

    def kept(merged):
        return lax.dynamic_index_in_dim(merged, chip, 0, keepdims=False)

    grad_wout = summed_chunks(
        [[kept(first_merged)] + first_parts, [kept(last_merged)] + last_parts]
    )
    grad_query = both_halves(dq_units[0], dq_other).astype(jnp.float32)
    summed = jnp.sum(
        dkv_all.reshape(count // 2, 2, tokens, 2 * HEAD_SIZE).astype(jnp.float32), 0
    )
    grad_key = jnp.concatenate([summed[0, :, :HEAD_SIZE], summed[1, :, :HEAD_SIZE]], 1)
    grad_value = jnp.concatenate([summed[0, :, HEAD_SIZE:], summed[1, :, HEAD_SIZE:]], 1)
    return (layer_out, grad_query, grad_key, grad_value, grad_wout)


def per_device(query_proj, projected_keys, projected_values, w_out, attended_blocks, grad_out):
    count, groups = lax.axis_size("ctx"), lax.axis_size("head")
    pairs = (
        projected_keys.shape[1] == 2 * HEAD_SIZE
        and query_proj.shape[0] == BLOCK_TOKENS
        and count >= 4
        and count & (count - 1) == 0
        and groups & (groups - 1) == 0
        and count % groups == 0
        and attended_blocks.shape[1] >= count
    )
    body = paired_device if pairs else general_device
    return body(
        query_proj, projected_keys, projected_values, w_out, attended_blocks, grad_out
    )


def solution(mesh):
    return jax.shard_map(
        per_device,
        mesh=mesh,
        in_specs=(
            P("ctx", "head"),
            P("ctx", "head"),
            P("ctx", "head"),
            P("head", None),
            P(),
            P("ctx", "head"),
        ),
        out_specs=(
            P("ctx", "head"),
            P("ctx", "head"),
            P("ctx", "head"),
            P("ctx", "head"),
            P("head", "ctx"),
        ),
        check_vma=False,
    )
```

```python
import functools
import math

import jax
import jax.numpy as jnp
from jax import lax
from jax.experimental import pallas as pl
from jax.experimental.pallas import tpu as pltpu
from jax.sharding import PartitionSpec as P

HEAD_SIZE = 128
BLOCK_TOKENS = 512


def shifted(value, axis, steps):
    count = lax.axis_size(axis)
    leading, last = (max(0, -steps), min(count, count - steps))
    return lax.ppermute(value, axis, [(source, source + steps) for source in range(leading, last)])


def load_key_block(source, local_index, kv_heads):
    rows_per_block = lax.dynamic_slice_in_dim(source, local_index * BLOCK_TOKENS, BLOCK_TOKENS, 0)
    return rows_per_block.reshape(BLOCK_TOKENS, kv_heads, HEAD_SIZE)


def causal_scores(query_portion, key_row_slice, key_block_index, diagonal_block):
    raw_scores = jnp.einsum(
        "ikgd,jkd->kgij", query_portion, key_row_slice, preferred_element_type=jnp.float32
    ) * HEAD_SIZE ** (-0.5)
    row_pos = lax.broadcasted_iota(jnp.int32, (BLOCK_TOKENS, BLOCK_TOKENS), 0)
    col_pos = lax.broadcasted_iota(jnp.int32, (BLOCK_TOKENS, BLOCK_TOKENS), 1)
    allowed = (key_block_index < diagonal_block) | (col_pos <= row_pos)
    return jnp.where(allowed, raw_scores, -jnp.inf)


def general_device(query_proj, projected_keys, projected_values, w_out, attended_blocks, grad_out):
    ctx_rank = lax.axis_index("ctx")
    ctx_count = lax.axis_size("ctx")
    local_rows = query_proj.shape[0]
    blocks_here = local_rows // BLOCK_TOKENS
    kv_heads = projected_keys.shape[1] // HEAD_SIZE
    key_column_span = projected_keys.shape[1]
    head_cols = query_proj.shape[1]
    heads_per_group = head_cols // HEAD_SIZE // kv_heads
    slot_count = attended_blocks.shape[1]
    score_scale = HEAD_SIZE ** (-0.5)
    reach = min((slot_count - 1 + blocks_here - 1) // blocks_here, ctx_count - 1)
    margin_rows = reach * local_rows
    far_step = ctx_count // 2
    use_far = far_step > reach
    window_rows = margin_rows + local_rows
    front_rows = max(reach, far_step) * local_rows
    all_keys, all_values = (
        lax.all_gather(projected_keys, "ctx", axis=0, tiled=True),
        lax.all_gather(projected_values, "ctx", axis=0, tiled=True),
    )
    total_rows = all_keys.shape[0]

    def heads_of(source):
        return source.reshape(BLOCK_TOKENS, kv_heads, heads_per_group, HEAD_SIZE)

    local_block = 0
    diagonal_block = ctx_rank * blocks_here + local_block
    listed = lax.dynamic_index_in_dim(attended_blocks, diagonal_block, 0, keepdims=False)
    query_portion = heads_of(query_proj)

    def forward_visit(slot_num, running):
        key_block_index = listed[slot_num]

        def forward_live(present_block):
            running_largest, softmax_denominator, weighted_values = present_block
            score_matrix = causal_scores(
                query_portion,
                load_key_block(all_keys, key_block_index, kv_heads),
                key_block_index,
                diagonal_block,
            )
            new_largest = jnp.maximum(running_largest, jnp.max(score_matrix, -1))
            rescale = jnp.exp(running_largest - new_largest)
            attention_weights = jnp.exp(score_matrix - new_largest[..., None])
            softmax_denominator = softmax_denominator * rescale + jnp.sum(attention_weights, -1)
            value_row_slice = load_key_block(all_values, key_block_index, kv_heads)
            weighted_values = weighted_values * rescale[..., None] + jnp.einsum(
                "mayf,fmb->mayb",
                attention_weights.astype(jnp.bfloat16),
                value_row_slice,
                preferred_element_type=jnp.float32,
            )
            return (new_largest, softmax_denominator, weighted_values)

        return lax.cond(
            key_block_index >= 0, forward_live, lambda present_block: present_block, running
        )

    initial_state = (
        jnp.full((kv_heads, heads_per_group, BLOCK_TOKENS), -jnp.inf, jnp.float32),
        jnp.zeros((kv_heads, heads_per_group, BLOCK_TOKENS), jnp.float32),
        jnp.zeros((kv_heads, heads_per_group, BLOCK_TOKENS, HEAD_SIZE), jnp.float32),
    )
    running_largest, softmax_denominator, weighted_values = lax.fori_loop(
        0, slot_count, forward_visit, initial_state
    )
    attn_block = (weighted_values / softmax_denominator[..., None]).astype(jnp.bfloat16)
    attn_parts = attn_block.transpose(2, 0, 1, 3).reshape(BLOCK_TOKENS, head_cols)
    log_totals = [running_largest + jnp.log(softmax_denominator)]
    out_terms = jnp.dot(attn_parts, w_out, preferred_element_type=jnp.float32)
    layer_out = lax.psum_scatter(
        out_terms.astype(jnp.bfloat16), "head", scatter_dimension=1, tiled=True
    )
    piece = lax.all_gather(grad_out, "head", axis=1, tiled=True)
    grad_sum = lax.dot_general(
        piece, w_out, (((1,), (1,)), ((), ())), preferred_element_type=jnp.float32
    )
    column_term = lax.dot_general(
        attn_parts, piece, (((0,), (0,)), ((), ())), preferred_element_type=jnp.float32
    )
    weight_terms = column_term
    grad_sum, weight_terms = (grad_sum, weight_terms)
    grad_attn = grad_sum.astype(jnp.bfloat16)
    grad_wout = lax.psum_scatter(
        weight_terms.astype(jnp.bfloat16), "ctx", scatter_dimension=1, tiled=True
    ).astype(jnp.float32)
    key_gradient_totals = jnp.zeros((total_rows, key_column_span), jnp.float32)
    value_gradient_totals = jnp.zeros((total_rows, key_column_span), jnp.float32)
    local_block = 0
    diagonal_block = ctx_rank * blocks_here + local_block
    listed = lax.dynamic_index_in_dim(attended_blocks, diagonal_block, 0, keepdims=False)
    query_portion = heads_of(query_proj)
    grad_heads = heads_of(grad_attn)
    attn_heads = heads_of(attn_parts)
    delta = jnp.einsum("ikgd,ikgd->kgi", grad_heads, attn_heads, preferred_element_type=jnp.float32)
    log_total = log_totals[local_block]

    def reverse_visit(slot_num, running):
        key_block_index = listed[slot_num]

        def reverse_live(present_block):
            query_gradient_total, key_buffer, value_buffer = present_block
            key_row_slice = load_key_block(all_keys, key_block_index, kv_heads)
            value_row_slice = load_key_block(all_values, key_block_index, kv_heads)
            score_matrix = causal_scores(
                query_portion, key_row_slice, key_block_index, diagonal_block
            )
            probs = jnp.exp(score_matrix - log_total[..., None])
            grad_probs = jnp.einsum(
                "ikgd,jkd->kgij", grad_heads, value_row_slice, preferred_element_type=jnp.float32
            )
            grad_scores = (score_scale * probs * (grad_probs - delta[..., None])).astype(
                jnp.bfloat16
            )
            query_gradient_total = query_gradient_total + jnp.einsum(
                "mayf,fmb->mayb", grad_scores, key_row_slice, preferred_element_type=jnp.float32
            )
            key_add = jnp.einsum(
                "kgij,ikgd->jkd", grad_scores, query_portion, preferred_element_type=jnp.float32
            ).reshape(BLOCK_TOKENS, -1)
            value_add = jnp.einsum(
                "kgij,ikgd->jkd",
                probs.astype(jnp.bfloat16),
                grad_heads,
                preferred_element_type=jnp.float32,
            ).reshape(BLOCK_TOKENS, -1)
            begin = key_block_index * BLOCK_TOKENS
            key_buffer = lax.dynamic_update_slice_in_dim(
                key_buffer,
                lax.dynamic_slice_in_dim(key_buffer, begin, BLOCK_TOKENS, 0) + key_add,
                begin,
                0,
            )
            value_buffer = lax.dynamic_update_slice_in_dim(
                value_buffer,
                lax.dynamic_slice_in_dim(value_buffer, begin, BLOCK_TOKENS, 0) + value_add,
                begin,
                0,
            )
            return (query_gradient_total, key_buffer, value_buffer)

        return lax.cond(
            key_block_index >= 0, reverse_live, lambda present_block: present_block, running
        )

    initial_state = (
        jnp.zeros((kv_heads, heads_per_group, BLOCK_TOKENS, HEAD_SIZE), jnp.float32),
        key_gradient_totals,
        value_gradient_totals,
    )
    query_gradient_total, key_gradient_totals, value_gradient_totals = lax.fori_loop(
        0, slot_count, reverse_visit, initial_state
    )
    query_grads = query_gradient_total.transpose(2, 0, 1, 3).reshape(BLOCK_TOKENS, head_cols)

    def to_window(buffer):
        padded = jnp.concatenate([jnp.zeros((front_rows, key_column_span), jnp.float32), buffer], 0)
        window_part = lax.dynamic_slice_in_dim(
            padded, front_rows - margin_rows + ctx_rank * local_rows, window_rows, 0
        )
        if use_far:
            far_part = lax.dynamic_slice_in_dim(
                padded, front_rows + (ctx_rank - far_step) * local_rows, local_rows, 0
            )
            return jnp.concatenate([window_part, far_part], 0)
        return window_part

    low_keys = to_window(key_gradient_totals).astype(jnp.bfloat16)
    low_values = to_window(value_gradient_totals).astype(jnp.bfloat16)
    grad_key = low_keys[margin_rows:window_rows].astype(jnp.float32)
    grad_value = low_values[margin_rows:window_rows].astype(jnp.float32)
    for distance in range(1, reach + 1):
        begin = (reach - distance) * local_rows
        back_keys, back_values = shifted(
            (low_keys[begin : begin + local_rows], low_values[begin : begin + local_rows]),
            "ctx",
            -distance,
        )
        grad_key = grad_key + back_keys.astype(jnp.float32)
        grad_value = grad_value + back_values.astype(jnp.float32)
    if use_far:
        far_back_keys, far_back_values = shifted(
            (low_keys[window_rows:], low_values[window_rows:]), "ctx", -far_step
        )
        grad_key = grad_key + far_back_keys.astype(jnp.float32)
        grad_value = grad_value + far_back_values.astype(jnp.float32)
    return (layer_out, query_grads, grad_key, grad_value, grad_wout)


MESH = pl.DeviceIdType.MESH
VMEM_BYTES = 48 * 1024 * 1024
EXP2_SCALE = HEAD_SIZE ** (-0.5) * math.log2(math.e)
CONTRACT_LAST = (((1,), (1,)), ((), ()))
CONTRACT_FIRST = (((0,), (0,)), ((), ()))


def dot(left, right, dims=(((1,), (0,)), ((), ()))):
    return lax.dot_general(left, right, dims, preferred_element_type=jnp.float32)


def remote(source, target, send_sem, recv_sem, axis, peer):
    return pltpu.make_async_remote_copy(
        src_ref=source,
        dst_ref=target,
        send_sem=send_sem,
        recv_sem=recv_sem,
        device_id={axis: peer},
        device_id_type=MESH,
    )


def exchange_kernel(
    count,
    groups,
    spread,
    blocks_ref,
    halves_ref,
    columns_ref,
    blocks_all,
    other,
    columns_all,
    send,
    recv,
    half,
    group_send,
    group_recv,
    local,
):
    me, group = lax.axis_index("ctx"), lax.axis_index("head")
    core = lax.rem(me, 2)
    width = columns_all.shape[1] // groups

    def columns_of(ref, index):
        return ref.at[:, pl.ds(pl.multiple_of(index * width, width), width)]

    barrier = pltpu.get_barrier_semaphore()
    for axis, rank, size in (("ctx", me, count), ("head", group, groups)):
        for step in range(1, size):
            pl.semaphore_signal(
                barrier,
                inc=1,
                device_id={axis: lax.rem(rank + step, size)},
                device_id_type=MESH,
            )
    pl.semaphore_wait(barrier, count + groups - 2)

    copies = []
    source = halves_ref.at[1 - core] if spread else halves_ref.at[1]
    copies.append(remote(source, other, half.at[0], half.at[1], "ctx", count - 1 - me))
    for step in range(1, groups):
        peer = lax.rem(group + step, groups)
        copies.append(
            remote(
                columns_ref if spread else columns_of(columns_ref, peer),
                columns_of(columns_all, group),
                group_send.at[step],
                group_recv.at[step],
                "head",
                peer,
            )
        )
    for step in range(1, count):
        peer = lax.rem(me + step, count)
        index = lax.rem(peer, 2) if spread else peer
        copies.append(
            remote(
                blocks_ref.at[index],
                blocks_all.at[me],
                send.at[step],
                recv.at[step],
                "ctx",
                peer,
            )
        )
    for copy in copies:
        copy.start()
    own = [
        pltpu.make_async_copy(blocks_ref.at[core if spread else me], blocks_all.at[me], local.at[0]),
        pltpu.make_async_copy(
            columns_ref if spread else columns_of(columns_ref, group),
            columns_of(columns_all, group),
            local.at[1],
        ),
    ]
    for copy in own:
        copy.start()
    for copy in own + copies:
        copy.wait()


def exchange(spread, collective_id, count, groups, blocks, units, columns):
    any_space = pl.BlockSpec(memory_space=pl.ANY)
    width = columns.shape[1] * (groups if spread else 1)
    return pl.pallas_call(
        functools.partial(exchange_kernel, count, groups, spread),
        out_shape=(
            jax.ShapeDtypeStruct((count,) + blocks.shape[1:], blocks.dtype),
            jax.ShapeDtypeStruct(units.shape[1:], units.dtype),
            jax.ShapeDtypeStruct((columns.shape[0], width), columns.dtype),
        ),
        in_specs=[any_space] * 3,
        out_specs=(any_space,) * 3,
        scratch_shapes=[
            pltpu.SemaphoreType.DMA((count,)),
            pltpu.SemaphoreType.DMA((count,)),
            pltpu.SemaphoreType.DMA((2,)),
            pltpu.SemaphoreType.DMA((groups,)),
            pltpu.SemaphoreType.DMA((groups,)),
            pltpu.SemaphoreType.DMA((2,)),
        ],
        compiler_params=pltpu.CompilerParams(
            collective_id=collective_id, has_side_effects=True, vmem_limit_bytes=VMEM_BYTES
        ),
        cost_estimate=pl.CostEstimate(
            flops=0, bytes_accessed=4 * blocks.size * 2 + units.size * 4, transcendentals=0
        ),
    )(blocks, units, columns)


def grad_attn_kernel(tiles, *refs):
    pieces, w_ref, out_ref = refs[:-2], refs[-2], refs[-1]
    width = w_ref.shape[1] // tiles // len(pieces)
    total = jnp.zeros(out_ref.shape, jnp.float32)
    for tile in range(tiles):
        for chunk, piece in enumerate(pieces):
            start = (tile * len(pieces) + chunk) * width
            total += dot(
                piece[:, tile * width : (tile + 1) * width],
                w_ref[:, start : start + width],
                CONTRACT_LAST,
            )
    out_ref[...] = total.astype(out_ref.dtype)


def grad_attn_of(pieces, w_out, tiles):
    tokens = pieces[0].shape[0]
    return pl.pallas_call(
        functools.partial(grad_attn_kernel, tiles),
        out_shape=jax.ShapeDtypeStruct((tokens, w_out.shape[0]), jnp.bfloat16),
        compiler_params=pltpu.CompilerParams(vmem_limit_bytes=VMEM_BYTES),
        cost_estimate=pl.CostEstimate(
            flops=2 * tokens * w_out.size, bytes_accessed=4 * w_out.size, transcendentals=0
        ),
    )(*pieces, w_out)


def out_terms_kernel(groups, attn_ref, w_ref, *out_refs):
    for group in range(groups):
        start = group * (w_ref.shape[1] // groups)
        for out_ref in out_refs:
            width = out_ref.shape[1] // groups
            out_ref[:, group * width : (group + 1) * width] = dot(
                attn_ref[...], w_ref[:, start : start + width]
            ).astype(out_ref.dtype)
            start += width


def out_terms_of(attn, w_out, groups, widths):
    tokens = attn.shape[0]
    return pl.pallas_call(
        functools.partial(out_terms_kernel, groups),
        out_shape=tuple(
            jax.ShapeDtypeStruct((tokens, groups * width), jnp.bfloat16) for width in widths
        ),
        compiler_params=pltpu.CompilerParams(vmem_limit_bytes=VMEM_BYTES),
        cost_estimate=pl.CostEstimate(
            flops=2 * tokens * w_out.size, bytes_accessed=4 * w_out.size, transcendentals=0
        ),
    )(attn, w_out)


def head_part(value, head):
    return value[:, head * HEAD_SIZE : (head + 1) * HEAD_SIZE]


def diagonal_mask(scores):
    key_row = lax.broadcasted_iota(jnp.int32, scores.shape, 0)
    query_col = lax.broadcasted_iota(jnp.int32, scores.shape, 1)
    return jnp.where(key_row <= query_col, scores, -jnp.inf)


def forward_kernel(rows_ref, q_ref, kv_ref, attn_ref, total_ref, largest, denominator, weighted):
    unit = pl.program_id(0)
    heads = q_ref.shape[2] // HEAD_SIZE

    def visit(block, diagonal):
        keys = kv_ref[block, :, :HEAD_SIZE]
        values = kv_ref[block, :, HEAD_SIZE:]
        for head in range(heads):
            at = pl.ds(head, 1)
            scores = dot(keys, head_part(q_ref[0], head), CONTRACT_LAST)
            if diagonal:
                scores = diagonal_mask(scores)
            top = jnp.max(scores, 0, keepdims=True)
            if not diagonal:
                before = largest[at, :]
                top = jnp.maximum(before, top)
                rescale = jnp.exp2((before - top) * EXP2_SCALE)
            weights = jnp.exp2(scores * EXP2_SCALE - top * EXP2_SCALE)
            added = jnp.sum(weights, 0, keepdims=True)
            product = dot(values, weights.astype(jnp.bfloat16), CONTRACT_FIRST)
            largest[at, :] = top
            if diagonal:
                denominator[at, :] = added
                weighted[head] = product
            else:
                denominator[at, :] = denominator[at, :] * rescale + added
                weighted[head] = weighted[head] * rescale + product

    visit(rows_ref[unit, 0], True)

    @pl.loop(1, rows_ref.shape[1])
    def _(slot):
        block = rows_ref[unit, slot]

        @pl.when(block >= 0)
        def _():
            visit(block, False)

    for head in range(heads):
        at = pl.ds(head, 1)
        bottom = denominator[at, :]
        attn_ref[0, :, head * HEAD_SIZE : (head + 1) * HEAD_SIZE] = (
            (weighted[head] / bottom).T.astype(jnp.bfloat16)
        )
        total_ref[0, at, :] = largest[at, :] * EXP2_SCALE + jnp.log2(bottom)


def forward_units(rows, q_units, kv_all):
    units, tokens, width = q_units.shape
    heads = width // HEAD_SIZE
    whole = pl.BlockSpec(kv_all.shape, lambda unit, rows: (0, 0, 0))
    per_unit = pl.BlockSpec((1, tokens, width), lambda unit, rows: (unit, 0, 0))
    per_total = pl.BlockSpec((1, heads, tokens), lambda unit, rows: (unit, 0, 0))
    return pl.pallas_call(
        forward_kernel,
        grid_spec=pltpu.PrefetchScalarGridSpec(
            num_scalar_prefetch=1,
            grid=(units,),
            in_specs=[per_unit, whole],
            out_specs=(per_unit, per_total),
            scratch_shapes=[
                pltpu.VMEM((heads, tokens), jnp.float32),
                pltpu.VMEM((heads, tokens), jnp.float32),
                pltpu.VMEM((heads, HEAD_SIZE, tokens), jnp.float32),
            ],
        ),
        out_shape=(
            jax.ShapeDtypeStruct(q_units.shape, jnp.bfloat16),
            jax.ShapeDtypeStruct((units, heads, tokens), jnp.float32),
        ),
        compiler_params=pltpu.CompilerParams(vmem_limit_bytes=VMEM_BYTES),
        cost_estimate=pl.CostEstimate(
            flops=20 * tokens * tokens * width,
            bytes_accessed=kv_all.size * 2,
            transcendentals=5 * tokens * tokens * heads,
        ),
    )(rows, q_units, kv_all)


def backward_kernel(
    rows_ref, q_ref, g_ref, attn_ref, total_ref, kv_ref, dq_ref, dkv_ref, delta, dq_sum, dkv_sum
):
    unit = pl.program_id(0)
    heads = q_ref.shape[2] // HEAD_SIZE
    score_scale = HEAD_SIZE ** (-0.5)

    @pl.when(unit == 0)
    def _():
        dkv_sum[...] = jnp.zeros_like(dkv_sum)

    for head in range(heads):
        product = head_part(g_ref[0], head).astype(jnp.float32) * head_part(
            attn_ref[0], head
        ).astype(jnp.float32)
        delta[pl.ds(head, 1), :] = jnp.sum(product.T, 0, keepdims=True)

    def visit(block, diagonal):
        keys = kv_ref[block, :, :HEAD_SIZE]
        values = kv_ref[block, :, HEAD_SIZE:]
        key_sum, value_sum = None, None
        for head in range(heads):
            at = pl.ds(head, 1)
            queries = head_part(q_ref[0], head)
            grads = head_part(g_ref[0], head)
            scores = dot(keys, queries, CONTRACT_LAST)
            if diagonal:
                scores = diagonal_mask(scores)
            probs = jnp.exp2(scores * EXP2_SCALE - total_ref[0, at, :])
            grad_probs = dot(values, grads, CONTRACT_LAST)
            grad_scores = (probs * (grad_probs - delta[at, :])).astype(jnp.bfloat16)
            value_add = dot(probs.astype(jnp.bfloat16), grads)
            key_add = dot(grad_scores, queries)
            query_add = dot(keys, grad_scores, CONTRACT_FIRST)
            dq_sum[head] = query_add if diagonal else dq_sum[head] + query_add
            key_sum = key_add if head == 0 else key_sum + key_add
            value_sum = value_add if head == 0 else value_sum + value_add
        dkv_sum[block, :, :HEAD_SIZE] += key_sum * score_scale
        dkv_sum[block, :, HEAD_SIZE:] += value_sum

    visit(rows_ref[unit, 0], True)

    @pl.loop(1, rows_ref.shape[1])
    def _(slot):
        block = rows_ref[unit, slot]

        @pl.when(block >= 0)
        def _():
            visit(block, False)

    for head in range(heads):
        dq_ref[0, :, head * HEAD_SIZE : (head + 1) * HEAD_SIZE] = (
            (dq_sum[head] * score_scale).T.astype(dq_ref.dtype)
        )

    @pl.when(unit == pl.num_programs(0) - 1)
    def _():
        dkv_ref[...] = dkv_sum[...].astype(dkv_ref.dtype)


def backward_units(rows, q_units, g_units, attn_units, totals, kv_all):
    units, tokens, width = q_units.shape
    heads = width // HEAD_SIZE
    whole = pl.BlockSpec(kv_all.shape, lambda unit, rows: (0, 0, 0))
    per_unit = pl.BlockSpec((1, tokens, width), lambda unit, rows: (unit, 0, 0))
    per_total = pl.BlockSpec((1, heads, tokens), lambda unit, rows: (unit, 0, 0))
    return pl.pallas_call(
        backward_kernel,
        grid_spec=pltpu.PrefetchScalarGridSpec(
            num_scalar_prefetch=1,
            grid=(units,),
            in_specs=[per_unit, per_unit, per_unit, per_total, whole],
            out_specs=(per_unit, whole),
            scratch_shapes=[
                pltpu.VMEM((heads, tokens), jnp.float32),
                pltpu.VMEM((heads, HEAD_SIZE, tokens), jnp.float32),
                pltpu.VMEM(kv_all.shape, jnp.float32),
            ],
        ),
        out_shape=(
            jax.ShapeDtypeStruct(q_units.shape, jnp.bfloat16),
            jax.ShapeDtypeStruct(kv_all.shape, jnp.bfloat16),
        ),
        compiler_params=pltpu.CompilerParams(vmem_limit_bytes=VMEM_BYTES),
        cost_estimate=pl.CostEstimate(
            flops=50 * tokens * tokens * width,
            bytes_accessed=kv_all.size * 4,
            transcendentals=5 * tokens * tokens * heads,
        ),
    )(rows, q_units, g_units, attn_units, totals, kv_all)


def halves_of(value):
    half = value.shape[1] // 2
    return jnp.stack([value[:, :half], value[:, half:]])


def swapped(value, count):
    return lax.ppermute(value, "ctx", [(c, count - 1 - c) for c in range(count)])


def merged_cores(terms, core, count):
    tiles = terms.reshape(count // 2, 2, terms.shape[0] // count, terms.shape[1])
    kept = jnp.where(core == 0, tiles[:, 0], tiles[:, 1])
    given = jnp.where(core == 0, tiles[:, 1], tiles[:, 0])
    taken = lax.ppermute(given, "ctx", [(c, c ^ 1) for c in range(count)])
    return (kept.astype(jnp.float32) + taken.astype(jnp.float32)).astype(jnp.bfloat16)


def chip_parts(merged, chip, count):
    parts = []
    for turn in range(1, count // 2):
        part = lax.dynamic_index_in_dim(merged, chip ^ turn, 0, keepdims=False)
        parts.append(lax.ppermute(part, "ctx", [(c, c ^ (2 * turn)) for c in range(count)]))
    return parts


def sum_kernel(*refs):
    out_ref = refs[-1]
    width = refs[0].shape[0]
    per_chunk = (len(refs) - 1) // (out_ref.shape[1] // width)
    for chunk in range(out_ref.shape[1] // width):
        total = refs[chunk * per_chunk][...].astype(jnp.float32)
        for ref in refs[chunk * per_chunk + 1 : (chunk + 1) * per_chunk]:
            total += ref[...].astype(jnp.float32)
        out_ref[:, chunk * width : (chunk + 1) * width] = total.T


def summed_chunks(chunks):
    width, rows = chunks[0][0].shape
    flat = [term for chunk in chunks for term in chunk]
    return pl.pallas_call(
        sum_kernel,
        out_shape=jax.ShapeDtypeStruct((rows, width * len(chunks)), jnp.float32),
        compiler_params=pltpu.CompilerParams(vmem_limit_bytes=VMEM_BYTES),
    )(*flat)


def column_chunk(value, tiles, chunk):
    width = value.shape[1] // tiles // 2
    starts = [(2 * tile + chunk) * width for tile in range(tiles)]
    return jnp.concatenate([value[:, start : start + width] for start in starts], 1)


def paired_device(query_proj, projected_keys, projected_values, w_out, attended_blocks, grad_out):
    count, groups = lax.axis_size("ctx"), lax.axis_size("head")
    me = lax.axis_index("ctx")
    core, chip = lax.rem(me, 2), lax.div(me, 2)
    tokens = query_proj.shape[0]
    own_tiles = count // groups
    chunks = [column_chunk(grad_out, own_tiles, chunk) for chunk in range(2)]
    last_piece = lax.all_gather(chunks[1], "head", axis=1, tiled=True)
    key_halves, value_halves = halves_of(projected_keys), halves_of(projected_values)

    def own_half(halves):
        return jnp.where(core == 0, halves[0], halves[1])

    def both_halves(own, other):
        return jnp.concatenate(
            [jnp.where(core == 0, own, other), jnp.where(core == 0, other, own)], 1
        )

    def weight_terms(piece, attn):
        terms = dot(piece, attn, CONTRACT_FIRST).astype(jnp.bfloat16)
        return merged_cores(terms, core, count)

    query_halves = halves_of(query_proj)
    kv_all, q_other, first_piece = exchange(
        True,
        0,
        count,
        groups,
        jnp.concatenate([key_halves, value_halves], 2),
        query_halves,
        chunks[0],
    )
    q_units = jnp.stack([own_half(query_halves), q_other])
    rows = jnp.take(attended_blocks, jnp.stack([me, count - 1 - me]), axis=0)
    attn_units, totals = forward_units(rows, q_units, kv_all)
    attn = both_halves(attn_units[0], swapped(attn_units[1], count))
    own_columns = grad_out.shape[1]
    direct = own_columns // 4
    scattered_terms, direct_terms = out_terms_of(
        attn, w_out, groups, (own_columns - direct, direct)
    )
    scattered = lax.psum_scatter(scattered_terms, "head", scatter_dimension=1, tiled=True)
    grad_attn = grad_attn_of([first_piece, last_piece], w_out, count)
    grad_halves = halves_of(grad_attn)
    grad_other = swapped(own_half(grad_halves[::-1]), count)
    g_units = jnp.stack([own_half(grad_halves), grad_other])
    first_piece, last_piece, direct_terms = lax.optimization_barrier(
        (first_piece, last_piece, direct_terms)
    )
    first_merged = weight_terms(first_piece, attn)
    last_merged = weight_terms(last_piece, attn)
    first_merged, last_merged, g_units = lax.optimization_barrier(
        (first_merged, last_merged, g_units)
    )
    first_parts = chip_parts(first_merged, chip, count)
    last_parts = chip_parts(last_merged, chip, count)
    dq_units, dkv = backward_units(rows, q_units, g_units, attn_units, totals, kv_all)
    first_parts, last_parts, dq_units, dkv = lax.optimization_barrier(
        (first_parts, last_parts, dq_units, dkv)
    )
    dkv_all, dq_other, direct_all = exchange(
        False, 1, count, groups, dkv, dq_units, direct_terms
    )
    direct_out = direct_all[:, :direct].astype(jnp.float32)
    for index in range(1, groups):
        direct_out += direct_all[:, index * direct : (index + 1) * direct].astype(jnp.float32)
    layer_out = jnp.concatenate([scattered, direct_out.astype(jnp.bfloat16)], 1)

    def kept(merged):
        return lax.dynamic_index_in_dim(merged, chip, 0, keepdims=False)

    grad_wout = summed_chunks(
        [[kept(first_merged)] + first_parts, [kept(last_merged)] + last_parts]
    )
    grad_query = both_halves(dq_units[0], dq_other).astype(jnp.float32)
    summed = jnp.sum(
        dkv_all.reshape(count // 2, 2, tokens, 2 * HEAD_SIZE).astype(jnp.float32), 0
    )
    grad_key = jnp.concatenate([summed[0, :, :HEAD_SIZE], summed[1, :, :HEAD_SIZE]], 1)
    grad_value = jnp.concatenate([summed[0, :, HEAD_SIZE:], summed[1, :, HEAD_SIZE:]], 1)
    return (layer_out, grad_query, grad_key, grad_value, grad_wout)


def per_device(query_proj, projected_keys, projected_values, w_out, attended_blocks, grad_out):
    count, groups = lax.axis_size("ctx"), lax.axis_size("head")
    pairs = (
        projected_keys.shape[1] == 2 * HEAD_SIZE
        and query_proj.shape[0] == BLOCK_TOKENS
        and count >= 4
        and count & (count - 1) == 0
        and groups & (groups - 1) == 0
        and count % groups == 0
        and attended_blocks.shape[1] >= count
    )
    body = paired_device if pairs else general_device
    return body(
        query_proj, projected_keys, projected_values, w_out, attended_blocks, grad_out
    )


def solution(mesh):
    return jax.shard_map(
        per_device,
        mesh=mesh,
        in_specs=(
            P("ctx", "head"),
            P("ctx", "head"),
            P("ctx", "head"),
            P("head", None),
            P(),
            P("ctx", "head"),
        ),
        out_specs=(
            P("ctx", "head"),
            P("ctx", "head"),
            P("ctx", "head"),
            P("ctx", "head"),
            P("head", "ctx"),
        ),
        check_vma=False,
    )
```

```python
import functools
import math

import jax
import jax.numpy as jnp
from jax import lax
from jax.experimental import pallas as pl
from jax.experimental.pallas import tpu as pltpu
from jax.sharding import PartitionSpec as P

HEAD_SIZE = 128
BLOCK_TOKENS = 512


def shifted(value, axis, steps):
    count = lax.axis_size(axis)
    leading, last = (max(0, -steps), min(count, count - steps))
    return lax.ppermute(value, axis, [(source, source + steps) for source in range(leading, last)])


def load_key_block(source, local_index, kv_heads):
    rows_per_block = lax.dynamic_slice_in_dim(source, local_index * BLOCK_TOKENS, BLOCK_TOKENS, 0)
    return rows_per_block.reshape(BLOCK_TOKENS, kv_heads, HEAD_SIZE)


def causal_scores(query_portion, key_row_slice, key_block_index, diagonal_block):
    raw_scores = jnp.einsum(
        "ikgd,jkd->kgij", query_portion, key_row_slice, preferred_element_type=jnp.float32
    ) * HEAD_SIZE ** (-0.5)
    row_pos = lax.broadcasted_iota(jnp.int32, (BLOCK_TOKENS, BLOCK_TOKENS), 0)
    col_pos = lax.broadcasted_iota(jnp.int32, (BLOCK_TOKENS, BLOCK_TOKENS), 1)
    allowed = (key_block_index < diagonal_block) | (col_pos <= row_pos)
    return jnp.where(allowed, raw_scores, -jnp.inf)


def general_device(query_proj, projected_keys, projected_values, w_out, attended_blocks, grad_out):
    ctx_rank = lax.axis_index("ctx")
    ctx_count = lax.axis_size("ctx")
    local_rows = query_proj.shape[0]
    blocks_here = local_rows // BLOCK_TOKENS
    kv_heads = projected_keys.shape[1] // HEAD_SIZE
    key_column_span = projected_keys.shape[1]
    head_cols = query_proj.shape[1]
    heads_per_group = head_cols // HEAD_SIZE // kv_heads
    slot_count = attended_blocks.shape[1]
    score_scale = HEAD_SIZE ** (-0.5)
    reach = min((slot_count - 1 + blocks_here - 1) // blocks_here, ctx_count - 1)
    margin_rows = reach * local_rows
    far_step = ctx_count // 2
    use_far = far_step > reach
    window_rows = margin_rows + local_rows
    front_rows = max(reach, far_step) * local_rows
    all_keys, all_values = (
        lax.all_gather(projected_keys, "ctx", axis=0, tiled=True),
        lax.all_gather(projected_values, "ctx", axis=0, tiled=True),
    )
    total_rows = all_keys.shape[0]

    def heads_of(source):
        return source.reshape(BLOCK_TOKENS, kv_heads, heads_per_group, HEAD_SIZE)

    local_block = 0
    diagonal_block = ctx_rank * blocks_here + local_block
    listed = lax.dynamic_index_in_dim(attended_blocks, diagonal_block, 0, keepdims=False)
    query_portion = heads_of(query_proj)

    def forward_visit(slot_num, running):
        key_block_index = listed[slot_num]

        def forward_live(present_block):
            running_largest, softmax_denominator, weighted_values = present_block
            score_matrix = causal_scores(
                query_portion,
                load_key_block(all_keys, key_block_index, kv_heads),
                key_block_index,
                diagonal_block,
            )
            new_largest = jnp.maximum(running_largest, jnp.max(score_matrix, -1))
            rescale = jnp.exp(running_largest - new_largest)
            attention_weights = jnp.exp(score_matrix - new_largest[..., None])
            softmax_denominator = softmax_denominator * rescale + jnp.sum(attention_weights, -1)
            value_row_slice = load_key_block(all_values, key_block_index, kv_heads)
            weighted_values = weighted_values * rescale[..., None] + jnp.einsum(
                "mayf,fmb->mayb",
                attention_weights.astype(jnp.bfloat16),
                value_row_slice,
                preferred_element_type=jnp.float32,
            )
            return (new_largest, softmax_denominator, weighted_values)

        return lax.cond(
            key_block_index >= 0, forward_live, lambda present_block: present_block, running
        )

    initial_state = (
        jnp.full((kv_heads, heads_per_group, BLOCK_TOKENS), -jnp.inf, jnp.float32),
        jnp.zeros((kv_heads, heads_per_group, BLOCK_TOKENS), jnp.float32),
        jnp.zeros((kv_heads, heads_per_group, BLOCK_TOKENS, HEAD_SIZE), jnp.float32),
    )
    running_largest, softmax_denominator, weighted_values = lax.fori_loop(
        0, slot_count, forward_visit, initial_state
    )
    attn_block = (weighted_values / softmax_denominator[..., None]).astype(jnp.bfloat16)
    attn_parts = attn_block.transpose(2, 0, 1, 3).reshape(BLOCK_TOKENS, head_cols)
    log_totals = [running_largest + jnp.log(softmax_denominator)]
    out_terms = jnp.dot(attn_parts, w_out, preferred_element_type=jnp.float32)
    layer_out = lax.psum_scatter(
        out_terms.astype(jnp.bfloat16), "head", scatter_dimension=1, tiled=True
    )
    piece = lax.all_gather(grad_out, "head", axis=1, tiled=True)
    grad_sum = lax.dot_general(
        piece, w_out, (((1,), (1,)), ((), ())), preferred_element_type=jnp.float32
    )
    column_term = lax.dot_general(
        attn_parts, piece, (((0,), (0,)), ((), ())), preferred_element_type=jnp.float32
    )
    weight_terms = column_term
    grad_sum, weight_terms = (grad_sum, weight_terms)
    grad_attn = grad_sum.astype(jnp.bfloat16)
    grad_wout = lax.psum_scatter(
        weight_terms.astype(jnp.bfloat16), "ctx", scatter_dimension=1, tiled=True
    ).astype(jnp.float32)
    key_gradient_totals = jnp.zeros((total_rows, key_column_span), jnp.float32)
    value_gradient_totals = jnp.zeros((total_rows, key_column_span), jnp.float32)
    local_block = 0
    diagonal_block = ctx_rank * blocks_here + local_block
    listed = lax.dynamic_index_in_dim(attended_blocks, diagonal_block, 0, keepdims=False)
    query_portion = heads_of(query_proj)
    grad_heads = heads_of(grad_attn)
    attn_heads = heads_of(attn_parts)
    delta = jnp.einsum("ikgd,ikgd->kgi", grad_heads, attn_heads, preferred_element_type=jnp.float32)
    log_total = log_totals[local_block]

    def reverse_visit(slot_num, running):
        key_block_index = listed[slot_num]

        def reverse_live(present_block):
            query_gradient_total, key_buffer, value_buffer = present_block
            key_row_slice = load_key_block(all_keys, key_block_index, kv_heads)
            value_row_slice = load_key_block(all_values, key_block_index, kv_heads)
            score_matrix = causal_scores(
                query_portion, key_row_slice, key_block_index, diagonal_block
            )
            probs = jnp.exp(score_matrix - log_total[..., None])
            grad_probs = jnp.einsum(
                "ikgd,jkd->kgij", grad_heads, value_row_slice, preferred_element_type=jnp.float32
            )
            grad_scores = (score_scale * probs * (grad_probs - delta[..., None])).astype(
                jnp.bfloat16
            )
            query_gradient_total = query_gradient_total + jnp.einsum(
                "mayf,fmb->mayb", grad_scores, key_row_slice, preferred_element_type=jnp.float32
            )
            key_add = jnp.einsum(
                "kgij,ikgd->jkd", grad_scores, query_portion, preferred_element_type=jnp.float32
            ).reshape(BLOCK_TOKENS, -1)
            value_add = jnp.einsum(
                "kgij,ikgd->jkd",
                probs.astype(jnp.bfloat16),
                grad_heads,
                preferred_element_type=jnp.float32,
            ).reshape(BLOCK_TOKENS, -1)
            begin = key_block_index * BLOCK_TOKENS
            key_buffer = lax.dynamic_update_slice_in_dim(
                key_buffer,
                lax.dynamic_slice_in_dim(key_buffer, begin, BLOCK_TOKENS, 0) + key_add,
                begin,
                0,
            )
            value_buffer = lax.dynamic_update_slice_in_dim(
                value_buffer,
                lax.dynamic_slice_in_dim(value_buffer, begin, BLOCK_TOKENS, 0) + value_add,
                begin,
                0,
            )
            return (query_gradient_total, key_buffer, value_buffer)

        return lax.cond(
            key_block_index >= 0, reverse_live, lambda present_block: present_block, running
        )

    initial_state = (
        jnp.zeros((kv_heads, heads_per_group, BLOCK_TOKENS, HEAD_SIZE), jnp.float32),
        key_gradient_totals,
        value_gradient_totals,
    )
    query_gradient_total, key_gradient_totals, value_gradient_totals = lax.fori_loop(
        0, slot_count, reverse_visit, initial_state
    )
    query_grads = query_gradient_total.transpose(2, 0, 1, 3).reshape(BLOCK_TOKENS, head_cols)

    def to_window(buffer):
        padded = jnp.concatenate([jnp.zeros((front_rows, key_column_span), jnp.float32), buffer], 0)
        window_part = lax.dynamic_slice_in_dim(
            padded, front_rows - margin_rows + ctx_rank * local_rows, window_rows, 0
        )
        if use_far:
            far_part = lax.dynamic_slice_in_dim(
                padded, front_rows + (ctx_rank - far_step) * local_rows, local_rows, 0
            )
            return jnp.concatenate([window_part, far_part], 0)
        return window_part

    low_keys = to_window(key_gradient_totals).astype(jnp.bfloat16)
    low_values = to_window(value_gradient_totals).astype(jnp.bfloat16)
    grad_key = low_keys[margin_rows:window_rows].astype(jnp.float32)
    grad_value = low_values[margin_rows:window_rows].astype(jnp.float32)
    for distance in range(1, reach + 1):
        begin = (reach - distance) * local_rows
        back_keys, back_values = shifted(
            (low_keys[begin : begin + local_rows], low_values[begin : begin + local_rows]),
            "ctx",
            -distance,
        )
        grad_key = grad_key + back_keys.astype(jnp.float32)
        grad_value = grad_value + back_values.astype(jnp.float32)
    if use_far:
        far_back_keys, far_back_values = shifted(
            (low_keys[window_rows:], low_values[window_rows:]), "ctx", -far_step
        )
        grad_key = grad_key + far_back_keys.astype(jnp.float32)
        grad_value = grad_value + far_back_values.astype(jnp.float32)
    return (layer_out, query_grads, grad_key, grad_value, grad_wout)


MESH = pl.DeviceIdType.MESH
VMEM_BYTES = 48 * 1024 * 1024
EXP2_SCALE = HEAD_SIZE ** (-0.5) * math.log2(math.e)
CONTRACT_LAST = (((1,), (1,)), ((), ()))
CONTRACT_FIRST = (((0,), (0,)), ((), ()))


def dot(left, right, dims=(((1,), (0,)), ((), ()))):
    return lax.dot_general(left, right, dims, preferred_element_type=jnp.float32)


def remote(source, target, send_sem, recv_sem, axis, peer):
    return pltpu.make_async_remote_copy(
        src_ref=source,
        dst_ref=target,
        send_sem=send_sem,
        recv_sem=recv_sem,
        device_id={axis: peer},
        device_id_type=MESH,
    )


def exchange_kernel(
    count,
    groups,
    spread,
    blocks_ref,
    halves_ref,
    columns_ref,
    blocks_all,
    other,
    columns_all,
    send,
    recv,
    half,
    group_send,
    group_recv,
    local,
):
    me = lax.axis_index("ctx")
    group = lax.axis_index("head") * min(groups - 1, 1)
    core = lax.rem(me, 2)
    width = columns_all.shape[1] // groups

    def columns_of(ref, index):
        return ref.at[:, pl.ds(pl.multiple_of(index * width, width), width)]

    barrier = pltpu.get_barrier_semaphore()
    for axis, rank, size in (("ctx", me, count), ("head", group, groups)):
        for step in range(1, size):
            pl.semaphore_signal(
                barrier,
                inc=1,
                device_id={axis: lax.rem(rank + step, size)},
                device_id_type=MESH,
            )
    pl.semaphore_wait(barrier, count + groups - 2)

    copies = []
    source = halves_ref.at[1 - core] if spread else halves_ref.at[1]
    copies.append(remote(source, other, half.at[0], half.at[1], "ctx", count - 1 - me))
    for step in range(1, groups):
        peer = lax.rem(group + step, groups)
        copies.append(
            remote(
                columns_ref if spread else columns_of(columns_ref, peer),
                columns_of(columns_all, group),
                group_send.at[step],
                group_recv.at[step],
                "head",
                peer,
            )
        )
    for step in range(1, count):
        peer = lax.rem(me + step, count)
        index = lax.rem(peer, 2) if spread else peer
        copies.append(
            remote(
                blocks_ref.at[index],
                blocks_all.at[me],
                send.at[step],
                recv.at[step],
                "ctx",
                peer,
            )
        )
    for copy in copies:
        copy.start()
    own = [
        pltpu.make_async_copy(blocks_ref.at[core if spread else me], blocks_all.at[me], local.at[0]),
        pltpu.make_async_copy(
            columns_ref if spread else columns_of(columns_ref, group),
            columns_of(columns_all, group),
            local.at[1],
        ),
    ]
    for copy in own:
        copy.start()
    for copy in own + copies:
        copy.wait()


def exchange(spread, collective_id, count, groups, blocks, units, columns):
    any_space = pl.BlockSpec(memory_space=pl.ANY)
    width = columns.shape[1] * (groups if spread else 1)
    return pl.pallas_call(
        functools.partial(exchange_kernel, count, groups, spread),
        out_shape=(
            jax.ShapeDtypeStruct((count,) + blocks.shape[1:], blocks.dtype),
            jax.ShapeDtypeStruct(units.shape[1:], units.dtype),
            jax.ShapeDtypeStruct((columns.shape[0], width), columns.dtype),
        ),
        in_specs=[any_space] * 3,
        out_specs=(any_space,) * 3,
        scratch_shapes=[
            pltpu.SemaphoreType.DMA((count,)),
            pltpu.SemaphoreType.DMA((count,)),
            pltpu.SemaphoreType.DMA((2,)),
            pltpu.SemaphoreType.DMA((groups,)),
            pltpu.SemaphoreType.DMA((groups,)),
            pltpu.SemaphoreType.DMA((2,)),
        ],
        compiler_params=pltpu.CompilerParams(
            collective_id=collective_id, has_side_effects=True, vmem_limit_bytes=VMEM_BYTES
        ),
        cost_estimate=pl.CostEstimate(
            flops=0, bytes_accessed=4 * blocks.size * 2 + units.size * 4, transcendentals=0
        ),
    )(blocks, units, columns)


def grad_attn_kernel(tiles, *refs):
    pieces, w_ref, out_ref = refs[:-2], refs[-2], refs[-1]
    width = w_ref.shape[1] // tiles // len(pieces)
    total = jnp.zeros(out_ref.shape, jnp.float32)
    for tile in range(tiles):
        for chunk, piece in enumerate(pieces):
            start = (tile * len(pieces) + chunk) * width
            total += dot(
                piece[:, tile * width : (tile + 1) * width],
                w_ref[:, start : start + width],
                CONTRACT_LAST,
            )
    out_ref[...] = total.astype(out_ref.dtype)


def grad_attn_of(pieces, w_out, tiles):
    tokens = pieces[0].shape[0]
    return pl.pallas_call(
        functools.partial(grad_attn_kernel, tiles),
        out_shape=jax.ShapeDtypeStruct((tokens, w_out.shape[0]), jnp.bfloat16),
        compiler_params=pltpu.CompilerParams(vmem_limit_bytes=VMEM_BYTES),
        cost_estimate=pl.CostEstimate(
            flops=2 * tokens * w_out.size, bytes_accessed=4 * w_out.size, transcendentals=0
        ),
    )(*pieces, w_out)


def out_terms_kernel(groups, attn_ref, w_ref, *out_refs):
    for group in range(groups):
        start = group * (w_ref.shape[1] // groups)
        for out_ref in out_refs:
            width = out_ref.shape[1] // groups
            out_ref[:, group * width : (group + 1) * width] = dot(
                attn_ref[...], w_ref[:, start : start + width]
            ).astype(out_ref.dtype)
            start += width


def out_terms_of(attn, w_out, groups, widths):
    tokens = attn.shape[0]
    return pl.pallas_call(
        functools.partial(out_terms_kernel, groups),
        out_shape=tuple(
            jax.ShapeDtypeStruct((tokens, groups * width), jnp.bfloat16) for width in widths
        ),
        compiler_params=pltpu.CompilerParams(vmem_limit_bytes=VMEM_BYTES),
        cost_estimate=pl.CostEstimate(
            flops=2 * tokens * w_out.size, bytes_accessed=4 * w_out.size, transcendentals=0
        ),
    )(attn, w_out)


def head_part(value, head):
    return value[:, head * HEAD_SIZE : (head + 1) * HEAD_SIZE]


def diagonal_mask(scores):
    key_row = lax.broadcasted_iota(jnp.int32, scores.shape, 0)
    query_col = lax.broadcasted_iota(jnp.int32, scores.shape, 1)
    return jnp.where(key_row <= query_col, scores, -jnp.inf)


def forward_kernel(rows_ref, q_ref, kv_ref, attn_ref, total_ref, largest, denominator, weighted):
    unit = pl.program_id(0)
    heads = q_ref.shape[2] // HEAD_SIZE

    def visit(block, diagonal):
        keys = kv_ref[block, :, :HEAD_SIZE]
        values = kv_ref[block, :, HEAD_SIZE:]
        for head in range(heads):
            at = pl.ds(head, 1)
            scores = dot(keys, head_part(q_ref[0], head), CONTRACT_LAST)
            if diagonal:
                scores = diagonal_mask(scores)
            top = jnp.max(scores, 0, keepdims=True)
            if not diagonal:
                before = largest[at, :]
                top = jnp.maximum(before, top)
                rescale = jnp.exp2((before - top) * EXP2_SCALE)
            weights = jnp.exp2(scores * EXP2_SCALE - top * EXP2_SCALE)
            added = jnp.sum(weights, 0, keepdims=True)
            product = dot(values, weights.astype(jnp.bfloat16), CONTRACT_FIRST)
            largest[at, :] = top
            if diagonal:
                denominator[at, :] = added
                weighted[head] = product
            else:
                denominator[at, :] = denominator[at, :] * rescale + added
                weighted[head] = weighted[head] * rescale + product

    visit(rows_ref[unit, 0], True)

    @pl.loop(1, rows_ref.shape[1])
    def _(slot):
        block = rows_ref[unit, slot]

        @pl.when(block >= 0)
        def _():
            visit(block, False)

    for head in range(heads):
        at = pl.ds(head, 1)
        bottom = denominator[at, :]
        attn_ref[0, :, head * HEAD_SIZE : (head + 1) * HEAD_SIZE] = (
            (weighted[head] / bottom).T.astype(jnp.bfloat16)
        )
        total_ref[0, at, :] = largest[at, :] * EXP2_SCALE + jnp.log2(bottom)


def forward_units(rows, q_units, kv_all):
    units, tokens, width = q_units.shape
    heads = width // HEAD_SIZE
    whole = pl.BlockSpec(kv_all.shape, lambda unit, rows: (0, 0, 0))
    per_unit = pl.BlockSpec((1, tokens, width), lambda unit, rows: (unit, 0, 0))
    per_total = pl.BlockSpec((1, heads, tokens), lambda unit, rows: (unit, 0, 0))
    return pl.pallas_call(
        forward_kernel,
        grid_spec=pltpu.PrefetchScalarGridSpec(
            num_scalar_prefetch=1,
            grid=(units,),
            in_specs=[per_unit, whole],
            out_specs=(per_unit, per_total),
            scratch_shapes=[
                pltpu.VMEM((heads, tokens), jnp.float32),
                pltpu.VMEM((heads, tokens), jnp.float32),
                pltpu.VMEM((heads, HEAD_SIZE, tokens), jnp.float32),
            ],
        ),
        out_shape=(
            jax.ShapeDtypeStruct(q_units.shape, jnp.bfloat16),
            jax.ShapeDtypeStruct((units, heads, tokens), jnp.float32),
        ),
        compiler_params=pltpu.CompilerParams(vmem_limit_bytes=VMEM_BYTES),
        cost_estimate=pl.CostEstimate(
            flops=20 * tokens * tokens * width,
            bytes_accessed=kv_all.size * 2,
            transcendentals=5 * tokens * tokens * heads,
        ),
    )(rows, q_units, kv_all)


def backward_kernel(
    rows_ref, q_ref, g_ref, attn_ref, total_ref, kv_ref, dq_ref, dkv_ref, delta, dq_sum, dkv_sum
):
    unit = pl.program_id(0)
    heads = q_ref.shape[2] // HEAD_SIZE
    score_scale = HEAD_SIZE ** (-0.5)

    @pl.when(unit == 0)
    def _():
        dkv_sum[...] = jnp.zeros_like(dkv_sum)

    for head in range(heads):
        product = head_part(g_ref[0], head).astype(jnp.float32) * head_part(
            attn_ref[0], head
        ).astype(jnp.float32)
        delta[pl.ds(head, 1), :] = jnp.sum(product.T, 0, keepdims=True)

    def visit(block, diagonal):
        keys = kv_ref[block, :, :HEAD_SIZE]
        values = kv_ref[block, :, HEAD_SIZE:]
        key_sum, value_sum = None, None
        for head in range(heads):
            at = pl.ds(head, 1)
            queries = head_part(q_ref[0], head)
            grads = head_part(g_ref[0], head)
            scores = dot(keys, queries, CONTRACT_LAST)
            if diagonal:
                scores = diagonal_mask(scores)
            probs = jnp.exp2(scores * EXP2_SCALE - total_ref[0, at, :])
            grad_probs = dot(values, grads, CONTRACT_LAST)
            grad_scores = (probs * (grad_probs - delta[at, :])).astype(jnp.bfloat16)
            value_add = dot(probs.astype(jnp.bfloat16), grads)
            key_add = dot(grad_scores, queries)
            query_add = dot(keys, grad_scores, CONTRACT_FIRST)
            dq_sum[head] = query_add if diagonal else dq_sum[head] + query_add
            key_sum = key_add if head == 0 else key_sum + key_add
            value_sum = value_add if head == 0 else value_sum + value_add
        dkv_sum[block, :, :HEAD_SIZE] += key_sum * score_scale
        dkv_sum[block, :, HEAD_SIZE:] += value_sum

    visit(rows_ref[unit, 0], True)

    @pl.loop(1, rows_ref.shape[1])
    def _(slot):
        block = rows_ref[unit, slot]

        @pl.when(block >= 0)
        def _():
            visit(block, False)

    for head in range(heads):
        dq_ref[0, :, head * HEAD_SIZE : (head + 1) * HEAD_SIZE] = (
            (dq_sum[head] * score_scale).T.astype(dq_ref.dtype)
        )

    @pl.when(unit == pl.num_programs(0) - 1)
    def _():
        dkv_ref[...] = dkv_sum[...].astype(dkv_ref.dtype)


def backward_units(rows, q_units, g_units, attn_units, totals, kv_all):
    units, tokens, width = q_units.shape
    heads = width // HEAD_SIZE
    whole = pl.BlockSpec(kv_all.shape, lambda unit, rows: (0, 0, 0))
    per_unit = pl.BlockSpec((1, tokens, width), lambda unit, rows: (unit, 0, 0))
    per_total = pl.BlockSpec((1, heads, tokens), lambda unit, rows: (unit, 0, 0))
    return pl.pallas_call(
        backward_kernel,
        grid_spec=pltpu.PrefetchScalarGridSpec(
            num_scalar_prefetch=1,
            grid=(units,),
            in_specs=[per_unit, per_unit, per_unit, per_total, whole],
            out_specs=(per_unit, whole),
            scratch_shapes=[
                pltpu.VMEM((heads, tokens), jnp.float32),
                pltpu.VMEM((heads, HEAD_SIZE, tokens), jnp.float32),
                pltpu.VMEM(kv_all.shape, jnp.float32),
            ],
        ),
        out_shape=(
            jax.ShapeDtypeStruct(q_units.shape, jnp.bfloat16),
            jax.ShapeDtypeStruct(kv_all.shape, jnp.bfloat16),
        ),
        compiler_params=pltpu.CompilerParams(vmem_limit_bytes=VMEM_BYTES),
        cost_estimate=pl.CostEstimate(
            flops=50 * tokens * tokens * width,
            bytes_accessed=kv_all.size * 4,
            transcendentals=5 * tokens * tokens * heads,
        ),
    )(rows, q_units, g_units, attn_units, totals, kv_all)


def halves_of(value):
    half = value.shape[1] // 2
    return jnp.stack([value[:, :half], value[:, half:]])


def swapped(value, count):
    return lax.ppermute(value, "ctx", [(c, count - 1 - c) for c in range(count)])


def merged_cores(terms, core, count):
    tiles = terms.reshape(count // 2, 2, terms.shape[0] // count, terms.shape[1])
    kept = jnp.where(core == 0, tiles[:, 0], tiles[:, 1])
    given = jnp.where(core == 0, tiles[:, 1], tiles[:, 0])
    taken = lax.ppermute(given, "ctx", [(c, c ^ 1) for c in range(count)])
    return (kept.astype(jnp.float32) + taken.astype(jnp.float32)).astype(jnp.bfloat16)


def chip_parts(merged, chip, count):
    parts = []
    for turn in range(1, count // 2):
        part = lax.dynamic_index_in_dim(merged, chip ^ turn, 0, keepdims=False)
        parts.append(lax.ppermute(part, "ctx", [(c, c ^ (2 * turn)) for c in range(count)]))
    return parts


def sum_kernel(*refs):
    out_ref = refs[-1]
    width = refs[0].shape[0]
    per_chunk = (len(refs) - 1) // (out_ref.shape[1] // width)
    for chunk in range(out_ref.shape[1] // width):
        total = refs[chunk * per_chunk][...].astype(jnp.float32)
        for ref in refs[chunk * per_chunk + 1 : (chunk + 1) * per_chunk]:
            total += ref[...].astype(jnp.float32)
        out_ref[:, chunk * width : (chunk + 1) * width] = total.T


def summed_chunks(chunks):
    width, rows = chunks[0][0].shape
    flat = [term for chunk in chunks for term in chunk]
    return pl.pallas_call(
        sum_kernel,
        out_shape=jax.ShapeDtypeStruct((rows, width * len(chunks)), jnp.float32),
        compiler_params=pltpu.CompilerParams(vmem_limit_bytes=VMEM_BYTES),
    )(*flat)


def paired_device(query_proj, projected_keys, projected_values, w_out, attended_blocks, grad_out):
    count, groups = lax.axis_size("ctx"), lax.axis_size("head")
    me = lax.axis_index("ctx")
    core, chip = lax.rem(me, 2), lax.div(me, 2)
    tokens = query_proj.shape[0]
    piece = lax.all_gather(grad_out, "head", axis=1, tiled=True)
    key_halves, value_halves = halves_of(projected_keys), halves_of(projected_values)

    def own_half(halves):
        return jnp.where(core == 0, halves[0], halves[1])

    def both_halves(own, other):
        return jnp.concatenate(
            [jnp.where(core == 0, own, other), jnp.where(core == 0, other, own)], 1
        )

    def weight_terms(piece, attn):
        terms = dot(piece, attn, CONTRACT_FIRST).astype(jnp.bfloat16)
        return merged_cores(terms, core, count)

    query_halves = halves_of(query_proj)
    kv_all, q_other, _ = exchange(
        True,
        0,
        count,
        1,
        jnp.concatenate([key_halves, value_halves], 2),
        query_halves,
        query_proj[:16, :HEAD_SIZE],
    )
    q_units = jnp.stack([own_half(query_halves), q_other])
    rows = jnp.take(attended_blocks, jnp.stack([me, count - 1 - me]), axis=0)
    attn_units, totals = forward_units(rows, q_units, kv_all)
    attn = both_halves(attn_units[0], swapped(attn_units[1], count))
    own_columns = grad_out.shape[1]
    direct = own_columns // 4
    scattered_terms, direct_terms = out_terms_of(
        attn, w_out, groups, (own_columns - direct, direct)
    )
    scattered = lax.psum_scatter(scattered_terms, "head", scatter_dimension=1, tiled=True)
    piece, direct_terms = lax.optimization_barrier((piece, direct_terms))
    grad_halves = halves_of(grad_attn_of([piece], w_out, count))
    piece, grad_halves = lax.optimization_barrier((piece, grad_halves))
    grad_other = swapped(own_half(grad_halves[::-1]), count)
    g_units = jnp.stack([own_half(grad_halves), grad_other])
    merged = weight_terms(piece, attn)
    merged, g_units = lax.optimization_barrier((merged, g_units))
    parts = chip_parts(merged, chip, count)
    dq_units, dkv = backward_units(rows, q_units, g_units, attn_units, totals, kv_all)
    parts, dq_units, dkv = lax.optimization_barrier((parts, dq_units, dkv))
    dkv_all, dq_other, direct_all = exchange(
        False, 1, count, groups, dkv, dq_units, direct_terms
    )
    direct_out = direct_all[:, :direct].astype(jnp.float32)
    for index in range(1, groups):
        direct_out += direct_all[:, index * direct : (index + 1) * direct].astype(jnp.float32)
    layer_out = jnp.concatenate([scattered, direct_out.astype(jnp.bfloat16)], 1)

    def kept(merged):
        return lax.dynamic_index_in_dim(merged, chip, 0, keepdims=False)

    grad_wout = summed_chunks([[kept(merged)] + parts])
    grad_query = both_halves(dq_units[0], dq_other).astype(jnp.float32)
    summed = jnp.sum(
        dkv_all.reshape(count // 2, 2, tokens, 2 * HEAD_SIZE).astype(jnp.float32), 0
    )
    grad_key = jnp.concatenate([summed[0, :, :HEAD_SIZE], summed[1, :, :HEAD_SIZE]], 1)
    grad_value = jnp.concatenate([summed[0, :, HEAD_SIZE:], summed[1, :, HEAD_SIZE:]], 1)
    return (layer_out, grad_query, grad_key, grad_value, grad_wout)


def per_device(query_proj, projected_keys, projected_values, w_out, attended_blocks, grad_out):
    count, groups = lax.axis_size("ctx"), lax.axis_size("head")
    pairs = (
        projected_keys.shape[1] == 2 * HEAD_SIZE
        and query_proj.shape[0] == BLOCK_TOKENS
        and count >= 4
        and count & (count - 1) == 0
        and groups & (groups - 1) == 0
        and count % groups == 0
        and attended_blocks.shape[1] >= count
    )
    body = paired_device if pairs else general_device
    return body(
        query_proj, projected_keys, projected_values, w_out, attended_blocks, grad_out
    )


def solution(mesh):
    return jax.shard_map(
        per_device,
        mesh=mesh,
        in_specs=(
            P("ctx", "head"),
            P("ctx", "head"),
            P("ctx", "head"),
            P("head", None),
            P(),
            P("ctx", "head"),
        ),
        out_specs=(
            P("ctx", "head"),
            P("ctx", "head"),
            P("ctx", "head"),
            P("ctx", "head"),
            P("head", "ctx"),
        ),
        check_vma=False,
    )
```
